32 devices in a mesh: row: 4 (over z), col: 4 (over y, core), depth: 2 (over x).
Axes of the slice: x: 2, y: 2, z: 4, core: 2. Of those that a mesh axis runs over, the one named last changes fastest.
Arguments:
- tokens: bfloat16 [256, 4096], P(('row', 'depth'), 'col'), may hold values from -6 to 6
- gate_weight: bfloat16 [4096, 14336], P('row', 'col'), may hold values from -0.09375 to 0.09375
- up_weight: bfloat16 [4096, 14336], P('row', 'col'), may hold values from -0.09375 to 0.09375
- grad_hidden: bfloat16 [256, 14336], P(('row', 'depth'), 'col'), may hold values from -6 to 6
Outputs:
- hidden: bfloat16 [256, 14336], P(('row', 'depth'), 'col')
- grad_tokens: bfloat16 [256, 4096], P(('col', 'depth'), 'row')
- grad_gate_weight: float32 [4096, 14336], P('row', ('col', 'depth'))
- grad_up_weight: float32 [4096, 14336], P('row', ('col', 'depth'))
The draws below stay inside these ranges and needn't reach their ends.
All inputs are finite; a program needn't handle non-finite values.
Results may differ from the reference program's by a relative error of at most 0.028.
Values may be sent and summed in bfloat16 or wider, within the bound.
A program may use at most 64 MiB of HBM per device.

```python
import jax
import jax.numpy as jnp
from jax import lax

D = 4096
FF = 14336
TOKENS = 256
N_ROW = 4
N_COL = 4


def levels(stream_key, shape, split, least, top_value):
    level, own = 1.0, jax.random.fold_in(stream_key, 6)
    for axis_at, blocks in split:
        steps = jnp.exp(jax.random.uniform(jax.random.fold_in(own, axis_at), (blocks,), jnp.float32, least / len(split), top_value / len(split)))
        level = level * jnp.repeat(steps, shape[axis_at] // blocks).reshape([-1 if axis == axis_at else 1 for axis in range(len(shape))])
    return level


def noise(stream_key, shape, width, most, shards=(), dtype=jnp.bfloat16):
    gain = levels(stream_key, shape, shards, -0.22, 0.18) if shards else 1.0
    values = jax.random.normal(stream_key, shape, jnp.float32) * width * gain
    return jnp.minimum(jnp.maximum(values, -most), most).astype(dtype)


def setup_inputs(seed: int = 0) -> dict:
    arg_keys = jax.random.split(jax.random.key(seed), 5)
    tokens = noise(arg_keys[0], (TOKENS, D), 1.0, 6.0, ((0, 8), (1, 4)))
    gate_weight = noise(arg_keys[1], (D, FF), D ** -0.5, 0.09375, ((0, 4), (1, 4)))
    up_weight = noise(arg_keys[2], (D, FF), D ** -0.5, 0.09375, ((0, 4), (1, 4)))
    grad_hidden = noise(arg_keys[3], (TOKENS, FF), 1.0, 6.0, ((0, 8), (1, 4)))
    return dict(tokens=tokens, gate_weight=gate_weight, up_weight=up_weight, grad_hidden=grad_hidden)


def local_grads(gate_pre, up_pre, cotangent):
    sigmoid_gate = jax.nn.sigmoid(gate_pre)
    cotan_f32 = cotangent.astype(jnp.float32)
    grad_gate = (cotan_f32 * up_pre * sigmoid_gate * (1.0 + gate_pre * (1.0 - sigmoid_gate))).astype(jnp.bfloat16)
    grad_up = (cotan_f32 * jax.nn.silu(gate_pre)).astype(jnp.bfloat16)
    return grad_gate, grad_up


def reference(tokens, gate_weight, up_weight, grad_hidden):
    feature_block = D // N_ROW
    gate_pre = jnp.zeros((tokens.shape[0], FF), jnp.float32)
    up_pre = jnp.zeros((tokens.shape[0], FF), jnp.float32)
    for block in range(N_ROW):
        first = block * feature_block
        last = first + feature_block
        gate_part = jnp.dot(tokens[:, first:last], gate_weight[first:last, :], preferred_element_type=jnp.float32)
        up_part = jnp.dot(tokens[:, first:last], up_weight[first:last, :], preferred_element_type=jnp.float32)
        gate_round = lax.optimization_barrier(gate_part.astype(jnp.bfloat16))
        up_round = lax.optimization_barrier(up_part.astype(jnp.bfloat16))
        gate_pre = gate_pre + gate_round.astype(jnp.float32)
        up_pre = up_pre + up_round.astype(jnp.float32)
    hidden = (jax.nn.silu(gate_pre) * up_pre).astype(jnp.bfloat16)
    grad_gate, grad_up = local_grads(gate_pre, up_pre, grad_hidden)
    block_cols = FF // N_COL
    total = jnp.zeros((tokens.shape[0], tokens.shape[1]), jnp.float32)
    for block in range(N_COL):
        column_start = block * block_cols
        column_end = column_start + block_cols
        part_sum = jnp.dot(grad_gate[:, column_start:column_end], gate_weight[:, column_start:column_end].T, preferred_element_type=jnp.float32)
        part_sum = part_sum + jnp.dot(grad_up[:, column_start:column_end], up_weight[:, column_start:column_end].T, preferred_element_type=jnp.float32)
        rounded = lax.optimization_barrier(part_sum.astype(jnp.bfloat16))
        total = total + rounded.astype(jnp.float32)
    grad_tokens = total.astype(jnp.bfloat16)
    grad_gate_weight = jnp.dot(tokens.T, grad_gate, preferred_element_type=jnp.float32)
    grad_up_weight = jnp.dot(tokens.T, grad_up, preferred_element_type=jnp.float32)
    return hidden, grad_tokens, grad_gate_weight, grad_up_weight
```

```python
import functools

import jax
import jax.numpy as jnp
from jax import lax
from jax.experimental import pallas as pl
from jax.experimental.pallas import tpu as pltpu
from jax.sharding import PartitionSpec as P

MESH = pl.DeviceIdType.MESH
LANES = 128
F32 = jnp.float32
BF16 = jnp.bfloat16


def aligned(start, size):
    return pl.ds(pl.multiple_of(start, size), size)


def kernel(
    tokens_ref, gate_ref, up_ref, cotan_ref,
    hidden_ref, grad_tokens_ref, every_tokens_ref, grad_gate_ref, grad_up_ref,
    tok, weights, sent, landed, to_peer, from_peer, own_sum, grads, cotan, hidden_rows,
    hidden_own, total, part, core_in, plane_out, plane_in,
    w_sem, tok_send, tok_recv, cotan_send, cotan_recv, cotan_local, sent_send, landed_recv,
    peer_send, peer_recv, grads_send, grads_recv, hidden_send, hidden_recv, out_sem,
    core_send, core_recv, plane_send, plane_recv,
):
    r, c, d = lax.axis_index("row"), lax.axis_index("col"), lax.axis_index("depth")
    other_d = 1 - d
    core = c + 1 - 2 * (c % 2)
    across = (c + 2) % 4
    pair = r + 1 - 2 * (r % 2)
    peer = 3 - r
    half = r // 2
    far = 1 - half
    chunks = weights.shape[0]
    width = chunks * LANES
    rows = tokens_ref.shape[0]
    block = 2 * rows
    group = 4 * rows

    def remote(src, dst, send, recv, **where):
        return pltpu.make_async_remote_copy(
            src_ref=src, dst_ref=dst, send_sem=send, recv_sem=recv,
            device_id={"row": r, "col": c, "depth": d, **where}, device_id_type=MESH,
        )

    def load(k, which):
        ref = (gate_ref, up_ref)[which]
        return pltpu.make_async_copy(
            ref.at[:, aligned(d * width + k * LANES, LANES)],
            weights.at[k, :, pl.ds(which * LANES, LANES)],
            w_sem.at[which, k],
        )

    @pl.loop(0, chunks)
    def _(k):
        load(k, 0).start()
        load(k, 1).start()

    barrier = pltpu.get_barrier_semaphore()
    partners = [dict(row=(r + step) % 4) for step in (1, 2, 3)] + [
        dict(row=pair, depth=other_d),
        dict(col=core),
        dict(col=across),
        dict(depth=other_d),
        dict(col=across, depth=other_d),
    ]
    for where in partners:
        pl.semaphore_signal(
            barrier, inc=1, device_id={"row": r, "col": c, "depth": d, **where},
            device_id_type=MESH,
        )
    pl.semaphore_wait(barrier, len(partners))

    def piece(row, depth):
        return tok.at[aligned(row * block + depth * rows, rows), :]

    is_root = c == r
    is_relay = across == r
    is_even = (c - r + 4) % 2 == 0

    def first_hop():
        return remote(
            tokens_ref, piece(r, d), tok_send.at[3, r * 2 + d], tok_recv.at[r * 2 + d], row=c
        )

    def forward(way, row, depth):
        where = (dict(col=across), dict(depth=other_d), dict(col=core))[way]
        at = row * 2 + depth
        return remote(
            piece(row, depth), piece(row, depth), tok_send.at[way, at], tok_recv.at[at], **where
        )

    def cotan_copy(depth, row):
        return remote(
            cotan_ref.at[:, aligned(depth * width, width)],
            cotan.at[aligned((r % 2) * block + d * rows, rows), :],
            cotan_send.at[depth], cotan_recv.at[(r % 2) * 2 + d], row=row, depth=depth,
        )

    def own_cotan():
        return pltpu.make_async_copy(
            cotan_ref.at[:, aligned(d * width, width)],
            cotan.at[aligned((r % 2) * block + d * rows, rows), :],
            cotan_local,
        )

    outer = (r == 0) | (r == 3)
    inner = (r == 1) | (r == 2)

    @pl.when(is_root)
    def _():
        tok[aligned(r * block + d * rows, rows), :] = tokens_ref[...]

    @pl.when(c != r)
    def _():
        first_hop().start()

    def near(step):
        row = (r + step) % 4

        def arrive():
            forward(0, row, d).wait_recv()

        if step == 0:
            pl.when(c != r)(arrive)
        else:
            arrive()

        @pl.when(is_root)
        def _():
            forward(0, row, d).start()

        @pl.when(is_even)
        def _():
            forward(1, row, d).start()
            forward(2, row, d).start()

    def away(step):
        row = (r + step) % 4
        forward(1, row, other_d).wait_recv()

        @pl.when(is_even)
        def _():
            forward(2, row, other_d).start()

    near(0)
    near(1)
    away(0)
    near(2)
    away(1)
    near(3)
    away(2)
    away(3)

    @pl.when(outer)
    def _():
        cotan_copy(d, pair).start()
        cotan_copy(other_d, pair).start()

    @pl.when(inner)
    def _():
        own_cotan().start()
        cotan_copy(other_d, r).start()

    def keep_tokens():
        return pltpu.make_async_copy(tok, every_tokens_ref, out_sem.at[0])

    keep_tokens().start()

    def partial(k, which):
        return jnp.dot(
            tok[aligned(which * group, group), :], weights[k], preferred_element_type=F32
        )

    def weight_wait(k):
        load(k, 0).wait()
        load(k, 1).wait()

    def keep(k, which, kind):
        ref = (grad_gate_ref, grad_up_ref)[kind]
        return pltpu.make_async_copy(
            grads.at[k, which, :, pl.ds(kind * LANES, LANES)],
            ref.at[aligned(which * group, group), aligned(k * LANES, LANES)],
            out_sem.at[1 + kind],
        )

    def add_tokens_grad(k):
        for which in range(2):
            keep(k, which, 0).start()
            keep(k, which, 1).start()
        left = grads[k].reshape(2 * group, 2 * LANES)
        step = min(256, total.shape[1])
        for at in range(0, total.shape[1], step):
            term = lax.dot_general(
                left, weights[k, pl.ds(at, step), :], (((1,), (1,)), ((), ())),
                preferred_element_type=F32,
            )
            total[:, pl.ds(at, step)] += term

    total[...] = jnp.zeros_like(total)

    def send_part(k, which):
        return remote(
            sent.at[k, which], landed.at[k, which], sent_send.at[k, which],
            landed_recv.at[k, which], row=pair,
        )

    def send_peer(k):
        return remote(to_peer.at[k], from_peer.at[k], peer_send.at[k], peer_recv.at[k], row=peer)

    def send_grads(k, which, to, way):
        return remote(
            grads.at[k, which], grads.at[k, which], grads_send.at[way, k],
            grads_recv.at[k, which], row=to,
        )

    def send_hidden(k, way):
        row, depth = ((r, other_d), (pair, d), (pair, other_d))[way]
        return remote(
            hidden_rows.at[
                aligned((row % 2) * block + depth * rows, rows), aligned(k * LANES, LANES)
            ],
            hidden_own.at[:, aligned(d * width + k * LANES, LANES)],
            hidden_send.at[way, k], hidden_recv.at[d], row=row, depth=depth,
        )

    def hidden_arrived(depth):
        return remote(
            hidden_rows.at[pl.ds(0, rows), :], hidden_own.at[:, aligned(depth * width, width)],
            hidden_send.at[0, 0], hidden_recv.at[depth],
        )

    @pl.when(outer)
    def _():
        @pl.loop(0, chunks)
        def _(k):
            weight_wait(k)

            @pl.when(k >= 2)
            def _():
                send_part(k - 2, far).wait_send()
                send_part(k - 2, half).wait_send()

            sent[k, far] = partial(k, far).astype(BF16)
            send_part(k, far).start()
            sent[k, half] = partial(k, half).astype(BF16)
            send_part(k, half).start()

        @pl.loop(chunks - 2, chunks)
        def _(k):
            send_part(k, far).wait_send()
            send_part(k, half).wait_send()

        @pl.loop(0, chunks)
        def _(k):
            send_grads(k, half, r, 0).wait_recv()
            send_grads(k, far, r, 0).wait_recv()
            add_tokens_grad(k)

        cotan_copy(d, pair).wait_send()
        cotan_copy(other_d, pair).wait_send()
        hidden_arrived(d).wait_recv()

    @pl.when(inner)
    def _():
        def reduce(k):
            weight_wait(k)
            mine = partial(k, far)
            send_part(k, far).wait_recv()
            to_peer[k] = (mine + landed[k, far].astype(F32)).astype(BF16)
            send_peer(k).start()
            mine = partial(k, half)
            send_part(k, half).wait_recv()
            own_sum[k] = mine + landed[k, half].astype(F32)

        def pointwise(k):
            @pl.when(k == 0)
            def _():
                own_cotan().wait()
                for row, depth in ((r, other_d), (pair, d), (pair, other_d)):
                    remote(
                        cotan_ref.at[:, pl.ds(0, width)],
                        cotan.at[aligned((row % 2) * block + depth * rows, rows), :],
                        cotan_send.at[0], cotan_recv.at[(row % 2) * 2 + depth],
                    ).wait_recv()

            send_peer(k).wait_recv()
            sums = own_sum[k] + from_peer[k].astype(F32)
            gate, up = sums[:, :LANES], sums[:, LANES:]
            cols = aligned(k * LANES, LANES)
            cot = cotan[:, cols].astype(F32)
            sigmoid = jax.nn.sigmoid(gate)
            silu = gate * sigmoid
            grads[k, half, :, pl.ds(0, LANES)] = (
                cot * up * sigmoid * (1.0 + gate * (1.0 - sigmoid))
            ).astype(BF16)
            grads[k, half, :, pl.ds(LANES, LANES)] = (cot * silu).astype(BF16)
            send_grads(k, half, peer, 0).start()
            send_grads(k, half, pair, 1).start()
            hidden_rows[:, cols] = (silu * up).astype(BF16)
            for way in range(3):
                send_hidden(k, way).start()
            hidden_own[:, aligned(d * width + k * LANES, LANES)] = hidden_rows[
                aligned((r % 2) * block + d * rows, rows), cols
            ]

        def spread(k):
            send_grads(k, far, pair, 2).wait_recv()
            send_grads(k, far, pair, 2).start()
            add_tokens_grad(k)

        @pl.loop(0, chunks + 2)
        def _(i):
            @pl.when(i < chunks)
            def _():
                reduce(i)

            @pl.when((i >= 1) & (i <= chunks))
            def _():
                pointwise(i - 1)

            @pl.when(i >= 2)
            def _():
                spread(i - 2)

        cotan_copy(other_d, r).wait_send()

    part[...] = total[...].astype(BF16)

    def core_copy(slot):
        col = (core, (core + 2) % 4)[slot]
        return remote(
            part.at[aligned(col * block, block), :], core_in.at[slot],
            core_send.at[slot], core_recv.at[slot], col=core,
        )

    core_copy(1).start()
    core_copy(0).start()

    def plane_copy(way):
        where = (
            dict(col=across, depth=other_d), dict(col=across), dict(depth=other_d)
        )[way]
        depth = (other_d, d, other_d)[way]
        slot = (1, 1, 0)[way]
        return remote(
            plane_out.at[slot, aligned(depth * rows, rows), :], plane_in.at[way],
            plane_send.at[way], plane_recv.at[way], **where,
        )

    core_copy(1).wait_recv()
    plane_out[1] = (
        total[aligned(across * block, block), :] + core_in[1].astype(F32)
    ).astype(BF16)
    plane_copy(0).start()
    plane_copy(1).start()
    core_copy(0).wait_recv()
    plane_out[0] = (
        total[aligned(c * block, block), :] + core_in[0].astype(F32)
    ).astype(BF16)
    plane_copy(2).start()

    hidden_arrived(other_d).wait_recv()
    hidden_ref[...] = hidden_own[...]

    @pl.when(c != r)
    def _():
        first_hop().wait_send()

    for row in range(4):
        @pl.when(is_root)
        def _():
            forward(0, row, d).wait_send()

        @pl.when(is_even)
        def _():
            forward(1, row, d).wait_send()
            forward(2, row, d).wait_send()
            forward(2, row, other_d).wait_send()

    @pl.when(inner)
    def _():
        @pl.loop(0, chunks)
        def _(k):
            send_peer(k).wait_send()
            send_grads(k, half, peer, 0).wait_send()
            send_grads(k, half, pair, 1).wait_send()
            send_grads(k, far, pair, 2).wait_send()
            for way in range(3):
                send_hidden(k, way).wait_send()

    keep_tokens().wait()
    pltpu.make_async_copy(grad_gate_ref, grad_gate_ref, out_sem.at[1]).wait()
    pltpu.make_async_copy(grad_up_ref, grad_up_ref, out_sem.at[2]).wait()
    core_copy(0).wait_send()
    core_copy(1).wait_send()
    own = plane_out[0, aligned(d * rows, rows), :].astype(F32)
    for way in range(3):
        plane_copy(way).wait_recv()
        own = own + plane_in[way].astype(F32)
    grad_tokens_ref[...] = own.astype(BF16)
    for way in range(3):
        plane_copy(way).wait_send()


def exchange(tokens, gate_weight, up_weight, grad_hidden):
    rows, feats = tokens.shape
    cols = gate_weight.shape[1]
    chunks = cols // (2 * LANES)
    every = 8 * rows
    group = every // 2
    dma = pltpu.SemaphoreType.DMA
    vmem = pl.BlockSpec(memory_space=pltpu.VMEM)
    hbm = pl.BlockSpec(memory_space=pl.ANY)
    scratch = [
        pltpu.VMEM((every, feats), BF16),
        pltpu.VMEM((chunks, feats, 2 * LANES), BF16),
        pltpu.VMEM((chunks, 2, group, 2 * LANES), BF16),
        pltpu.VMEM((chunks, 2, group, 2 * LANES), BF16),
        pltpu.VMEM((chunks, group, 2 * LANES), BF16),
        pltpu.VMEM((chunks, group, 2 * LANES), BF16),
        pltpu.VMEM((chunks, group, 2 * LANES), F32),
        pltpu.VMEM((chunks, 2, group, 2 * LANES), BF16),
        pltpu.VMEM((group, cols // 2), BF16),
        pltpu.VMEM((group, cols // 2), BF16),
        pltpu.VMEM((rows, cols), BF16),
        pltpu.VMEM((every, feats), F32),
        pltpu.VMEM((every, feats), BF16),
        pltpu.VMEM((2, 2 * rows, feats), BF16),
        pltpu.VMEM((2, 2 * rows, feats), BF16),
        pltpu.VMEM((3, rows, feats), BF16),
        dma((2, chunks)),
        dma((4, 8)),
        dma((8,)),
        dma((2,)),
        dma((4,)),
        dma,
        dma((chunks, 2)),
        dma((chunks, 2)),
        dma((chunks,)),
        dma((chunks,)),
        dma((3, chunks)),
        dma((chunks, 2)),
        dma((3, chunks)),
        dma((2,)),
        dma((3,)),
        dma((2,)),
        dma((2,)),
        dma((3,)),
        dma((3,)),
    ]
    return pl.pallas_call(
        kernel,
        out_shape=(
            jax.ShapeDtypeStruct((rows, cols), BF16),
            jax.ShapeDtypeStruct((rows, feats), BF16),
            jax.ShapeDtypeStruct((every, feats), BF16),
            jax.ShapeDtypeStruct((every, cols // 2), BF16),
            jax.ShapeDtypeStruct((every, cols // 2), BF16),
        ),
        in_specs=[vmem, hbm, hbm, vmem],
        out_specs=(vmem, vmem, hbm, hbm, hbm),
        scratch_shapes=scratch,
        compiler_params=pltpu.CompilerParams(
            collective_id=0, has_side_effects=True, vmem_limit_bytes=44 * 2**20
        ),
        cost_estimate=pl.CostEstimate(
            flops=8 * every * feats * cols // 2, bytes_accessed=4 * feats * cols,
            transcendentals=group * cols // 2,
        ),
    )(tokens, gate_weight, up_weight, grad_hidden)


def on_line(tokens, gate_weight, up_weight, grad_hidden):
    hidden, grad_tokens, every_tokens, grad_gate, grad_up = exchange(
        tokens, gate_weight, up_weight, grad_hidden
    )
    grad_gate_weight = jnp.einsum("td,tf->df", every_tokens, grad_gate, preferred_element_type=F32)
    grad_up_weight = jnp.einsum("td,tf->df", every_tokens, grad_up, preferred_element_type=F32)
    return (hidden, grad_tokens, grad_gate_weight, grad_up_weight)


def from_root(value, axis, source):
    kept = jnp.where(lax.axis_index(axis) == source, value, 0).astype(value.dtype)
    return lax.psum(kept, axis)


def local_grads(gate_pre, up_pre, cotangent):
    sigmoid_gate = jax.nn.sigmoid(gate_pre)
    cotan_f32 = cotangent.astype(jnp.float32)
    grad_gate = (
        cotan_f32 * up_pre * sigmoid_gate * (1.0 + gate_pre * (1.0 - sigmoid_gate))
    ).astype(jnp.bfloat16)
    grad_up = (cotan_f32 * jax.nn.silu(gate_pre)).astype(jnp.bfloat16)
    return (grad_gate, grad_up)


def matmul_f32(left, right):
    return jnp.dot(left, right, preferred_element_type=jnp.float32)


def rounded_term(left, right):
    return matmul_f32(left, right).astype(jnp.bfloat16).astype(jnp.float32)


def local(tokens, gate_weight, up_weight, grad_hidden):
    hidden_cols = gate_weight.shape[1]
    row_tokens = lax.all_gather(tokens, "row", axis=0, tiled=True)
    diag_panel = from_root(row_tokens, "col", lax.axis_index("row"))
    summed = lax.psum_scatter(
        jnp.concatenate(
            [rounded_term(diag_panel, gate_weight), rounded_term(diag_panel, up_weight)], 1
        ).astype(jnp.bfloat16),
        "row",
        scatter_dimension=0,
        tiled=True,
    ).astype(jnp.float32)
    gate_sum = summed[:, :hidden_cols]
    up_sum = summed[:, hidden_cols:]
    hidden = (jax.nn.silu(gate_sum) * up_sum).astype(jnp.bfloat16)
    own_gate, own_up = local_grads(gate_sum, up_sum, grad_hidden)
    grad_gate, grad_up = (
        lax.all_gather(own_gate, "row", axis=0, tiled=True),
        lax.all_gather(own_up, "row", axis=0, tiled=True),
    )
    first_term = jnp.einsum("tf,df->td", grad_gate, gate_weight, preferred_element_type=jnp.float32)
    grad_tokens = lax.psum_scatter(
        (
            first_term
            + jnp.einsum("tf,df->td", grad_up, up_weight, preferred_element_type=jnp.float32)
        ).astype(jnp.bfloat16),
        "col",
        scatter_dimension=0,
        tiled=True,
    )
    gate_slices, up_slices = (
        lax.all_to_all(grad_gate, "depth", split_axis=1, concat_axis=0, tiled=True),
        lax.all_to_all(grad_up, "depth", split_axis=1, concat_axis=0, tiled=True),
    )
    every_tokens = lax.all_gather(diag_panel, "depth", axis=0, tiled=True)
    grad_gate_weight = jnp.einsum(
        "td,tf->df", every_tokens, gate_slices, preferred_element_type=jnp.float32
    )
    grad_up_weight = jnp.einsum(
        "td,tf->df", every_tokens, up_slices, preferred_element_type=jnp.float32
    )
    return (hidden, grad_tokens, grad_gate_weight, grad_up_weight)


def pick(mesh, tokens, gate_weight, up_weight, grad_hidden):
    sizes = dict(mesh.shape)
    fits = (
        (sizes["row"], sizes["col"], sizes["depth"]) == (4, 4, 2)
        and tokens.shape[0] % 16 == 0
        and tokens.shape[1] % 128 == 0
        and gate_weight.shape[1] % (2 * LANES) == 0
    )
    plan = on_line if fits else local
    return plan(tokens, gate_weight, up_weight, grad_hidden)


def solution(mesh):
    return jax.shard_map(
        functools.partial(pick, mesh),
        mesh=mesh,
        in_specs=(
            P(("row", "depth"), "col"),
            P("row", "col"),
            P("row", "col"),
            P(("row", "depth"), "col"),
        ),
        out_specs=(
            P(("row", "depth"), "col"),
            P(("col", "depth"), "row"),
            P("row", ("col", "depth")),
            P("row", ("col", "depth")),
        ),
        check_vma=False,
    )
```

```python
import functools

import jax
import jax.numpy as jnp
from jax import lax
from jax.experimental import pallas as pl
from jax.experimental.pallas import tpu as pltpu
from jax.sharding import PartitionSpec as P

MESH = pl.DeviceIdType.MESH
LANES = 128
F32 = jnp.float32
BF16 = jnp.bfloat16


def aligned(start, size):
    return pl.ds(pl.multiple_of(start, size), size)


def kernel(
    tokens_ref, gate_ref, up_ref, cotan_ref,
    hidden_ref, grad_tokens_ref, every_tokens_ref, grad_gate_ref, grad_up_ref,
    tok, turned, weights, sent, landed, to_peer, from_peer, own_sum, grads, cotan, hidden_rows,
    hidden_own, total, part, core_in, plane_out, plane_in,
    w_sem, tok_send, tok_recv, cotan_send, cotan_recv, cotan_local, own_sem, sent_send, landed_recv,
    peer_send, peer_recv, grads_send, grads_recv, hidden_send, hidden_recv, out_sem,
    core_send, core_recv, plane_send, plane_recv,
):
    r, c, d = lax.axis_index("row"), lax.axis_index("col"), lax.axis_index("depth")
    other_d = 1 - d
    core = c + 1 - 2 * (c % 2)
    across = (c + 2) % 4
    pair = r + 1 - 2 * (r % 2)
    peer = 3 - r
    half = r // 2
    far = 1 - half
    chunks = weights.shape[0]
    width = chunks * LANES
    rows = tokens_ref.shape[0]
    block = 2 * rows
    group = 4 * rows

    def remote(src, dst, send, recv, **where):
        return pltpu.make_async_remote_copy(
            src_ref=src, dst_ref=dst, send_sem=send, recv_sem=recv,
            device_id={"row": r, "col": c, "depth": d, **where}, device_id_type=MESH,
        )

    def load(k, which):
        ref = (gate_ref, up_ref)[which]
        return pltpu.make_async_copy(
            ref.at[:, aligned(d * width + k * LANES, LANES)],
            weights.at[k, :, pl.ds(which * LANES, LANES)],
            w_sem.at[which, k],
        )

    @pl.loop(0, chunks)
    def _(k):
        load(k, 0).start()
        load(k, 1).start()

    barrier = pltpu.get_barrier_semaphore()
    partners = [dict(row=(r + step) % 4) for step in (1, 2, 3)] + [
        dict(row=pair, depth=other_d),
        dict(col=core),
        dict(col=across),
        dict(depth=other_d),
        dict(col=across, depth=other_d),
    ]
    for where in partners:
        pl.semaphore_signal(
            barrier, inc=1, device_id={"row": r, "col": c, "depth": d, **where},
            device_id_type=MESH,
        )
    pl.semaphore_wait(barrier, len(partners))

    def piece(row, depth):
        return tok.at[aligned(row * block + depth * rows, rows), :]

    is_root = c == r
    is_relay = across == r
    is_even = (c - r + 4) % 2 == 0

    def first_hop():
        return remote(
            tokens_ref, piece(r, d), tok_send.at[3, r * 2 + d], tok_recv.at[r * 2 + d], row=c
        )

    def forward(way, row, depth):
        where = (dict(col=across), dict(depth=other_d), dict(col=core))[way]
        at = row * 2 + depth
        return remote(
            piece(row, depth), piece(row, depth), tok_send.at[way, at], tok_recv.at[at], **where
        )

    def cotan_copy(depth, row):
        return remote(
            cotan_ref.at[:, aligned(depth * width, width)],
            cotan.at[aligned((r % 2) * block + d * rows, rows), :],
            cotan_send.at[depth], cotan_recv.at[(r % 2) * 2 + d], row=row, depth=depth,
        )

    def own_cotan():
        return pltpu.make_async_copy(
            cotan_ref.at[:, aligned(d * width, width)],
            cotan.at[aligned((r % 2) * block + d * rows, rows), :],
            cotan_local,
        )

    outer = (r == 0) | (r == 3)
    inner = (r == 1) | (r == 2)

    def own_tokens():
        return pltpu.make_async_copy(tokens_ref, piece(r, d), own_sem)

    @pl.when(c != r)
    def _():
        first_hop().start()

    @pl.when(is_root)
    def _():
        own_tokens().start()
        own_tokens().wait()

    order = (r, pair, 3 - pair, peer)

    def near(step):
        row = order[step]

        def arrive():
            forward(0, row, d).wait_recv()

        if step == 0:
            pl.when(c != r)(arrive)
        else:
            arrive()

        @pl.when(is_root)
        def _():
            forward(0, row, d).start()

        @pl.when(is_even)
        def _():
            forward(1, row, d).start()
            forward(2, row, d).start()

    def away(step):
        row = order[step]
        forward(1, row, other_d).wait_recv()

        @pl.when(is_even)
        def _():
            forward(2, row, other_d).start()

    def partial(k, which):
        return jnp.dot(
            tok[aligned(which * group, group), :], weights[k], preferred_element_type=F32
        )

    def weight_wait(k):
        load(k, 0).wait()
        load(k, 1).wait()

    def send_part(k, which):
        return remote(
            sent.at[k, which], landed.at[k, which], sent_send.at[k, which],
            landed_recv.at[k, which], row=pair,
        )

    near(0)
    near(1)

    @pl.when(outer)
    def _():
        cotan_copy(d, pair).start()
        cotan_copy(other_d, pair).start()

    @pl.when(inner)
    def _():
        own_cotan().start()
        cotan_copy(other_d, r).start()

    away(0)
    away(1)

    @pl.when(outer)
    def _():
        weight_wait(0)
        sent[0, half] = partial(0, half).astype(BF16)
        send_part(0, half).start()

    near(2)
    away(2)
    near(3)
    away(3)

    def keep_tokens():
        return pltpu.make_async_copy(turned, every_tokens_ref, out_sem.at[0])

    def keep(k, which, kind):
        ref = (grad_gate_ref, grad_up_ref)[kind]
        return pltpu.make_async_copy(
            grads.at[k, which, :, pl.ds(kind * LANES, LANES)],
            ref.at[aligned(which * group, group), aligned(k * LANES, LANES)],
            out_sem.at[1 + kind],
        )

    def add_tokens_grad(k):
        for which in range(2):
            keep(k, which, 0).start()
            keep(k, which, 1).start()
        left = grads[k].reshape(2 * group, 2 * LANES)
        step = min(256, total.shape[1])
        for at in range(0, total.shape[1], step):
            term = lax.dot_general(
                left, weights[k, pl.ds(at, step), :], (((1,), (1,)), ((), ())),
                preferred_element_type=F32,
            )
            total[:, pl.ds(at, step)] += term

    total[...] = jnp.zeros_like(total)

    def send_peer(k):
        return remote(to_peer.at[k], from_peer.at[k], peer_send.at[k], peer_recv.at[k], row=peer)

    def send_grads(k, which, to, way):
        return remote(
            grads.at[k, which], grads.at[k, which], grads_send.at[way, k],
            grads_recv.at[k, which], row=to,
        )

    def send_hidden(way):
        row, depth = ((r, other_d), (pair, d), (pair, other_d))[way]
        return remote(
            hidden_rows.at[aligned((row % 2) * block + depth * rows, rows), :],
            hidden_own.at[:, aligned(d * width, width)],
            hidden_send.at[way], hidden_recv.at[d], row=row, depth=depth,
        )

    def hidden_arrived(depth):
        return remote(
            hidden_rows.at[pl.ds(0, rows), :], hidden_own.at[:, aligned(depth * width, width)],
            hidden_send.at[0], hidden_recv.at[depth],
        )

    @pl.when(outer)
    def _():
        @pl.loop(0, chunks)
        def _(k):
            @pl.when(k >= 1)
            def _():
                weight_wait(k)

            @pl.when(k >= 2)
            def _():
                send_part(k - 2, far).wait_send()
                send_part(k - 2, half).wait_send()

            sent[k, far] = partial(k, far).astype(BF16)
            send_part(k, far).start()

            @pl.when(k >= 1)
            def _():
                sent[k, half] = partial(k, half).astype(BF16)
                send_part(k, half).start()

        @pl.loop(chunks - 2, chunks)
        def _(k):
            send_part(k, far).wait_send()
            send_part(k, half).wait_send()

        @pl.loop(0, chunks)
        def _(k):
            send_grads(k, half, r, 0).wait_recv()
            send_grads(k, far, r, 0).wait_recv()
            add_tokens_grad(k)

        cotan_copy(d, pair).wait_send()
        cotan_copy(other_d, pair).wait_send()

    @pl.when(inner)
    def _():
        def reduce(k):
            weight_wait(k)
            mine = partial(k, far)
            send_part(k, far).wait_recv()
            to_peer[k] = (mine + landed[k, far].astype(F32)).astype(BF16)
            send_peer(k).start()
            mine = partial(k, half)
            send_part(k, half).wait_recv()
            own_sum[k] = mine + landed[k, half].astype(F32)

        def pointwise(k):
            @pl.when(k == 0)
            def _():
                own_cotan().wait()
                for row, depth in ((r, other_d), (pair, d), (pair, other_d)):
                    remote(
                        cotan_ref.at[:, pl.ds(0, width)],
                        cotan.at[aligned((row % 2) * block + depth * rows, rows), :],
                        cotan_send.at[0], cotan_recv.at[(row % 2) * 2 + depth],
                    ).wait_recv()

            send_peer(k).wait_recv()
            sums = own_sum[k] + from_peer[k].astype(F32)
            gate, up = sums[:, :LANES], sums[:, LANES:]
            cols = aligned(k * LANES, LANES)
            cot = cotan[:, cols].astype(F32)
            sigmoid = jax.nn.sigmoid(gate)
            silu = gate * sigmoid
            grads[k, half, :, pl.ds(0, LANES)] = (
                cot * up * sigmoid * (1.0 + gate * (1.0 - sigmoid))
            ).astype(BF16)
            grads[k, half, :, pl.ds(LANES, LANES)] = (cot * silu).astype(BF16)
            send_grads(k, half, peer, 0).start()
            send_grads(k, half, pair, 1).start()
            hidden_rows[:, cols] = (silu * up).astype(BF16)
            hidden_own[:, aligned(d * width + k * LANES, LANES)] = hidden_rows[
                aligned((r % 2) * block + d * rows, rows), cols
            ]

            @pl.when(k == chunks - 1)
            def _():
                send_hidden(0).start()

        def spread(k):
            send_grads(k, far, pair, 2).wait_recv()
            send_grads(k, far, pair, 2).start()

            @pl.when(k == chunks - 1)
            def _():
                send_hidden(1).start()
                send_hidden(2).start()

            add_tokens_grad(k)

        @pl.loop(0, chunks + 2)
        def _(i):
            @pl.when(i < chunks)
            def _():
                reduce(i)

            @pl.when((i >= 1) & (i <= chunks))
            def _():
                pointwise(i - 1)

            @pl.when(i >= 2)
            def _():
                spread(i - 2)

        cotan_copy(other_d, r).wait_send()

    part[...] = total[...].astype(BF16)

    def core_copy(slot):
        col = (core, (core + 2) % 4)[slot]
        return remote(
            part.at[aligned(col * block, block), :], core_in.at[slot],
            core_send.at[slot], core_recv.at[slot], col=core,
        )

    core_copy(1).start()
    core_copy(0).start()
    turned[...] = tok[...].T
    keep_tokens().start()

    def plane_copy(way):
        where = (
            dict(col=across, depth=other_d), dict(col=across), dict(depth=other_d)
        )[way]
        depth = (other_d, d, other_d)[way]
        slot = (1, 1, 0)[way]
        return remote(
            plane_out.at[slot, aligned(depth * rows, rows), :], plane_in.at[way],
            plane_send.at[way], plane_recv.at[way], **where,
        )

    core_copy(1).wait_recv()
    plane_out[1] = (
        total[aligned(across * block, block), :] + core_in[1].astype(F32)
    ).astype(BF16)
    plane_copy(0).start()
    plane_copy(1).start()
    core_copy(0).wait_recv()
    plane_out[0] = (
        total[aligned(c * block, block), :] + core_in[0].astype(F32)
    ).astype(BF16)
    plane_copy(2).start()

    @pl.when(outer)
    def _():
        hidden_arrived(d).wait_recv()

    hidden_arrived(other_d).wait_recv()
    hidden_ref[...] = hidden_own[...]

    @pl.when(c != r)
    def _():
        first_hop().wait_send()

    for row in range(4):
        @pl.when(is_root)
        def _():
            forward(0, row, d).wait_send()

        @pl.when(is_even)
        def _():
            forward(1, row, d).wait_send()
            forward(2, row, d).wait_send()
            forward(2, row, other_d).wait_send()

    @pl.when(inner)
    def _():
        @pl.loop(0, chunks)
        def _(k):
            send_peer(k).wait_send()
            send_grads(k, half, peer, 0).wait_send()
            send_grads(k, half, pair, 1).wait_send()
            send_grads(k, far, pair, 2).wait_send()

        for way in range(3):
            send_hidden(way).wait_send()

    keep_tokens().wait()
    pltpu.make_async_copy(grad_gate_ref, grad_gate_ref, out_sem.at[1]).wait()
    pltpu.make_async_copy(grad_up_ref, grad_up_ref, out_sem.at[2]).wait()
    core_copy(0).wait_send()
    core_copy(1).wait_send()
    own = plane_out[0, aligned(d * rows, rows), :].astype(F32)
    for way in range(3):
        plane_copy(way).wait_recv()
        own = own + plane_in[way].astype(F32)
    grad_tokens_ref[...] = own.astype(BF16)
    for way in range(3):
        plane_copy(way).wait_send()


def exchange(tokens, gate_weight, up_weight, grad_hidden):
    rows, feats = tokens.shape
    cols = gate_weight.shape[1]
    chunks = cols // (2 * LANES)
    every = 8 * rows
    group = every // 2
    dma = pltpu.SemaphoreType.DMA
    vmem = pl.BlockSpec(memory_space=pltpu.VMEM)
    hbm = pl.BlockSpec(memory_space=pl.ANY)
    scratch = [
        pltpu.VMEM((every, feats), BF16),
        pltpu.VMEM((feats, every), BF16),
        pltpu.VMEM((chunks, feats, 2 * LANES), BF16),
        pltpu.VMEM((chunks, 2, group, 2 * LANES), BF16),
        pltpu.VMEM((chunks, 2, group, 2 * LANES), BF16),
        pltpu.VMEM((chunks, group, 2 * LANES), BF16),
        pltpu.VMEM((chunks, group, 2 * LANES), BF16),
        pltpu.VMEM((chunks, group, 2 * LANES), F32),
        pltpu.VMEM((chunks, 2, group, 2 * LANES), BF16),
        pltpu.VMEM((group, cols // 2), BF16),
        pltpu.VMEM((group, cols // 2), BF16),
        pltpu.VMEM((rows, cols), BF16),
        pltpu.VMEM((every, feats), F32),
        pltpu.VMEM((every, feats), BF16),
        pltpu.VMEM((2, 2 * rows, feats), BF16),
        pltpu.VMEM((2, 2 * rows, feats), BF16),
        pltpu.VMEM((3, rows, feats), BF16),
        dma((2, chunks)),
        dma((4, 8)),
        dma((8,)),
        dma((2,)),
        dma((4,)),
        dma,
        dma,
        dma((chunks, 2)),
        dma((chunks, 2)),
        dma((chunks,)),
        dma((chunks,)),
        dma((3, chunks)),
        dma((chunks, 2)),
        dma((3,)),
        dma((2,)),
        dma((3,)),
        dma((2,)),
        dma((2,)),
        dma((3,)),
        dma((3,)),
    ]
    return pl.pallas_call(
        kernel,
        out_shape=(
            jax.ShapeDtypeStruct((rows, cols), BF16),
            jax.ShapeDtypeStruct((rows, feats), BF16),
            jax.ShapeDtypeStruct((feats, every), BF16),
            jax.ShapeDtypeStruct((every, cols // 2), BF16),
            jax.ShapeDtypeStruct((every, cols // 2), BF16),
        ),
        in_specs=[hbm, hbm, hbm, hbm],
        out_specs=(vmem, vmem, hbm, hbm, hbm),
        scratch_shapes=scratch,
        compiler_params=pltpu.CompilerParams(
            collective_id=0, has_side_effects=True, vmem_limit_bytes=60 * 2**20
        ),
        cost_estimate=pl.CostEstimate(
            flops=8 * every * feats * cols // 2, bytes_accessed=4 * feats * cols,
            transcendentals=group * cols // 2,
        ),
    )(tokens, gate_weight, up_weight, grad_hidden)


def weight_kernel(tokens_ref, gate_ref, up_ref, gate_out, up_out):
    tokens = tokens_ref[...]
    gate_out[...] = jnp.dot(tokens, gate_ref[...], preferred_element_type=F32)
    up_out[...] = jnp.dot(tokens, up_ref[...], preferred_element_type=F32)


def weight_grads(turned_tokens, grad_gate, grad_up):
    feats, every = turned_tokens.shape
    cols = grad_gate.shape[1]
    step = 2 * LANES if cols % (2 * LANES) == 0 else LANES
    grads = pl.BlockSpec((every, step), lambda at: (0, at))
    out = pl.BlockSpec((feats, step), lambda at: (0, at))
    shape = jax.ShapeDtypeStruct((feats, cols), F32)
    return pl.pallas_call(
        weight_kernel,
        grid=(cols // step,),
        out_shape=(shape, shape),
        in_specs=[pl.BlockSpec((feats, every), lambda at: (0, 0)), grads, grads],
        out_specs=(out, out),
        compiler_params=pltpu.CompilerParams(vmem_limit_bytes=60 * 2**20),
        cost_estimate=pl.CostEstimate(
            flops=4 * every * feats * cols, bytes_accessed=8 * feats * cols, transcendentals=0
        ),
    )(turned_tokens, grad_gate, grad_up)


def on_line(tokens, gate_weight, up_weight, grad_hidden):
    hidden, grad_tokens, turned_tokens, grad_gate, grad_up = exchange(
        tokens, gate_weight, up_weight, grad_hidden
    )
    return (hidden, grad_tokens, *weight_grads(turned_tokens, grad_gate, grad_up))


def from_root(value, axis, source):
    kept = jnp.where(lax.axis_index(axis) == source, value, 0).astype(value.dtype)
    return lax.psum(kept, axis)


def local_grads(gate_pre, up_pre, cotangent):
    sigmoid_gate = jax.nn.sigmoid(gate_pre)
    cotan_f32 = cotangent.astype(jnp.float32)
    grad_gate = (
        cotan_f32 * up_pre * sigmoid_gate * (1.0 + gate_pre * (1.0 - sigmoid_gate))
    ).astype(jnp.bfloat16)
    grad_up = (cotan_f32 * jax.nn.silu(gate_pre)).astype(jnp.bfloat16)
    return (grad_gate, grad_up)


def matmul_f32(left, right):
    return jnp.dot(left, right, preferred_element_type=jnp.float32)


def rounded_term(left, right):
    return matmul_f32(left, right).astype(jnp.bfloat16).astype(jnp.float32)


def local(tokens, gate_weight, up_weight, grad_hidden):
    hidden_cols = gate_weight.shape[1]
    row_tokens = lax.all_gather(tokens, "row", axis=0, tiled=True)
    diag_panel = from_root(row_tokens, "col", lax.axis_index("row"))
    summed = lax.psum_scatter(
        jnp.concatenate(
            [rounded_term(diag_panel, gate_weight), rounded_term(diag_panel, up_weight)], 1
        ).astype(jnp.bfloat16),
        "row",
        scatter_dimension=0,
        tiled=True,
    ).astype(jnp.float32)
    gate_sum = summed[:, :hidden_cols]
    up_sum = summed[:, hidden_cols:]
    hidden = (jax.nn.silu(gate_sum) * up_sum).astype(jnp.bfloat16)
    own_gate, own_up = local_grads(gate_sum, up_sum, grad_hidden)
    grad_gate, grad_up = (
        lax.all_gather(own_gate, "row", axis=0, tiled=True),
        lax.all_gather(own_up, "row", axis=0, tiled=True),
    )
    first_term = jnp.einsum("tf,df->td", grad_gate, gate_weight, preferred_element_type=jnp.float32)
    grad_tokens = lax.psum_scatter(
        (
            first_term
            + jnp.einsum("tf,df->td", grad_up, up_weight, preferred_element_type=jnp.float32)
        ).astype(jnp.bfloat16),
        "col",
        scatter_dimension=0,
        tiled=True,
    )
    gate_slices, up_slices = (
        lax.all_to_all(grad_gate, "depth", split_axis=1, concat_axis=0, tiled=True),
        lax.all_to_all(grad_up, "depth", split_axis=1, concat_axis=0, tiled=True),
    )
    every_tokens = lax.all_gather(diag_panel, "depth", axis=0, tiled=True)
    grad_gate_weight = jnp.einsum(
        "td,tf->df", every_tokens, gate_slices, preferred_element_type=jnp.float32
    )
    grad_up_weight = jnp.einsum(
        "td,tf->df", every_tokens, up_slices, preferred_element_type=jnp.float32
    )
    return (hidden, grad_tokens, grad_gate_weight, grad_up_weight)


def pick(mesh, tokens, gate_weight, up_weight, grad_hidden):
    sizes = dict(mesh.shape)
    fits = (
        (sizes["row"], sizes["col"], sizes["depth"]) == (4, 4, 2)
        and tokens.shape[0] % 16 == 0
        and tokens.shape[1] % 128 == 0
        and gate_weight.shape[1] % (2 * LANES) == 0
    )
    plan = on_line if fits else local
    return plan(tokens, gate_weight, up_weight, grad_hidden)


def solution(mesh):
    return jax.shard_map(
        functools.partial(pick, mesh),
        mesh=mesh,
        in_specs=(
            P(("row", "depth"), "col"),
            P("row", "col"),
            P("row", "col"),
            P(("row", "depth"), "col"),
        ),
        out_specs=(
            P(("row", "depth"), "col"),
            P(("col", "depth"), "row"),
            P("row", ("col", "depth")),
            P("row", ("col", "depth")),
        ),
        check_vma=False,
    )
```

```python
import functools

import jax
import jax.numpy as jnp
from jax import lax
from jax.experimental import pallas as pl
from jax.experimental.pallas import tpu as pltpu
from jax.sharding import PartitionSpec as P

MESH = pl.DeviceIdType.MESH
LANES = 128
F32 = jnp.float32
BF16 = jnp.bfloat16


def aligned(start, size):
    return pl.ds(pl.multiple_of(start, size), size)


def kernel(
    tokens_ref, gate_ref, up_ref, cotan_ref,
    hidden_ref, grad_tokens_ref, every_tokens_ref, grad_gate_ref, grad_up_ref,
    tok, turned, weights, sent, landed, to_peer, from_peer, own_sum, grads, cotan, hidden_rows,
    hidden_own, total, part, core_in, plane_out, plane_in,
    w_sem, tok_send, tok_recv, cotan_send, cotan_recv, cotan_local, own_sem, sent_send, landed_recv,
    peer_send, peer_recv, grads_send, grads_recv, hidden_send, hidden_recv, out_sem,
    core_send, core_recv, plane_send, plane_recv,
):
    r, c, d = lax.axis_index("row"), lax.axis_index("col"), lax.axis_index("depth")
    other_d = 1 - d
    core = c + 1 - 2 * (c % 2)
    across = (c + 2) % 4
    pair = r + 1 - 2 * (r % 2)
    peer = 3 - r
    half = r // 2
    far = 1 - half
    chunks = weights.shape[0]
    width = chunks * LANES
    rows = tokens_ref.shape[0]
    block = 2 * rows
    group = 4 * rows

    def remote(src, dst, send, recv, **where):
        return pltpu.make_async_remote_copy(
            src_ref=src, dst_ref=dst, send_sem=send, recv_sem=recv,
            device_id={"row": r, "col": c, "depth": d, **where}, device_id_type=MESH,
        )

    def load(k, which):
        ref = (gate_ref, up_ref)[which]
        return pltpu.make_async_copy(
            ref.at[:, aligned(d * width + k * LANES, LANES)],
            weights.at[k, :, pl.ds(which * LANES, LANES)],
            w_sem.at[which, k],
        )

    @pl.loop(0, chunks)
    def _(k):
        load(k, 0).start()
        load(k, 1).start()

    barrier = pltpu.get_barrier_semaphore()
    partners = [dict(row=(r + step) % 4) for step in (1, 2, 3)] + [
        dict(row=pair, depth=other_d),
        dict(col=core),
        dict(col=across),
        dict(depth=other_d),
        dict(col=across, depth=other_d),
    ]
    for where in partners:
        pl.semaphore_signal(
            barrier, inc=1, device_id={"row": r, "col": c, "depth": d, **where},
            device_id_type=MESH,
        )
    pl.semaphore_wait(barrier, len(partners))

    def piece(row, depth):
        return tok.at[aligned(row * block + depth * rows, rows), :]

    is_root = c == r
    is_relay = across == r
    is_even = (c - r + 4) % 2 == 0

    def first_hop():
        return remote(
            tokens_ref, piece(r, d), tok_send.at[3, r * 2 + d], tok_recv.at[r * 2 + d], row=c
        )

    def forward(way, row, depth):
        where = (dict(col=across), dict(depth=other_d), dict(col=core))[way]
        at = row * 2 + depth
        return remote(
            piece(row, depth), piece(row, depth), tok_send.at[way, at], tok_recv.at[at], **where
        )

    def cotan_copy(depth, row):
        return remote(
            cotan_ref.at[:, aligned(depth * width, width)],
            cotan.at[aligned((r % 2) * block + d * rows, rows), :],
            cotan_send.at[depth], cotan_recv.at[(r % 2) * 2 + d], row=row, depth=depth,
        )

    def own_cotan():
        return pltpu.make_async_copy(
            cotan_ref.at[:, aligned(d * width, width)],
            cotan.at[aligned((r % 2) * block + d * rows, rows), :],
            cotan_local,
        )

    outer = (r == 0) | (r == 3)
    inner = (r == 1) | (r == 2)

    def own_tokens():
        return pltpu.make_async_copy(tokens_ref, piece(r, d), own_sem)

    @pl.when(c != r)
    def _():
        first_hop().start()

    @pl.when(is_root)
    def _():
        own_tokens().start()
        own_tokens().wait()

    order = (r, pair, 3 - pair, peer)

    def near(step):
        row = order[step]

        def arrive():
            forward(0, row, d).wait_recv()

        if step == 0:
            pl.when(c != r)(arrive)
        else:
            arrive()

        @pl.when(is_root)
        def _():
            forward(0, row, d).start()

        @pl.when(is_even)
        def _():
            forward(1, row, d).start()
            forward(2, row, d).start()

    def away(step):
        row = order[step]
        forward(1, row, other_d).wait_recv()

        @pl.when(is_even)
        def _():
            forward(2, row, other_d).start()

    def partial(k, which):
        return jnp.dot(
            tok[aligned(which * group, group), :], weights[k], preferred_element_type=F32
        )

    def weight_wait(k):
        load(k, 0).wait()
        load(k, 1).wait()

    def send_part(k, which):
        return remote(
            sent.at[k, which], landed.at[k, which], sent_send.at[k, which],
            landed_recv.at[k, which], row=pair,
        )

    near(0)
    near(1)

    @pl.when(outer)
    def _():
        cotan_copy(d, pair).start()
        cotan_copy(other_d, pair).start()

    @pl.when(inner)
    def _():
        own_cotan().start()
        cotan_copy(other_d, r).start()

    away(0)
    away(1)

    @pl.when(outer)
    def _():
        weight_wait(0)
        sent[0, half] = partial(0, half).astype(BF16)
        send_part(0, half).start()

    near(2)
    away(2)
    near(3)
    away(3)

    def keep_tokens():
        return pltpu.make_async_copy(turned, every_tokens_ref, out_sem.at[0])

    def keep(k, which, kind):
        ref = (grad_gate_ref, grad_up_ref)[kind]
        return pltpu.make_async_copy(
            grads.at[k, which, :, pl.ds(kind * LANES, LANES)],
            ref.at[aligned(which * group, group), aligned(k * LANES, LANES)],
            out_sem.at[1 + kind],
        )

    def add_tokens_grad(k):
        for which in range(2):
            keep(k, which, 0).start()
            keep(k, which, 1).start()
        left = grads[k].reshape(2 * group, 2 * LANES)
        step = min(256, total.shape[1])
        for at in range(0, total.shape[1], step):
            term = lax.dot_general(
                left, weights[k, pl.ds(at, step), :], (((1,), (1,)), ((), ())),
                preferred_element_type=F32,
            )
            total[:, pl.ds(at, step)] += term

    total[...] = jnp.zeros_like(total)

    def send_peer(k):
        return remote(to_peer.at[k], from_peer.at[k], peer_send.at[k], peer_recv.at[k], row=peer)

    def send_grads(k, which, to, way):
        return remote(
            grads.at[k, which], grads.at[k, which], grads_send.at[way, k],
            grads_recv.at[k, which], row=to,
        )

    def send_hidden(way):
        row, depth = ((r, other_d), (pair, d), (pair, other_d))[way]
        return remote(
            hidden_rows.at[aligned((row % 2) * block + depth * rows, rows), :],
            hidden_own.at[:, aligned(d * width, width)],
            hidden_send.at[way], hidden_recv.at[d], row=row, depth=depth,
        )

    def hidden_arrived(depth):
        return remote(
            hidden_rows.at[pl.ds(0, rows), :], hidden_own.at[:, aligned(depth * width, width)],
            hidden_send.at[0], hidden_recv.at[depth],
        )

    def take_grads(k):
        send_grads(k, half, r, 0).wait_recv()
        send_grads(k, far, r, 0).wait_recv()
        add_tokens_grad(k)

    lag = min(6, chunks)

    @pl.when(outer)
    def _():
        @pl.loop(0, chunks)
        def _(k):
            @pl.when(k >= 1)
            def _():
                weight_wait(k)

            @pl.when(k >= 2)
            def _():
                send_part(k - 2, far).wait_send()
                send_part(k - 2, half).wait_send()

            sent[k, far] = partial(k, far).astype(BF16)
            send_part(k, far).start()

            @pl.when(k >= 1)
            def _():
                sent[k, half] = partial(k, half).astype(BF16)
                send_part(k, half).start()

            @pl.when(k >= lag)
            def _():
                take_grads(k - lag)

        @pl.loop(chunks - lag, chunks)
        def _(k):
            take_grads(k)

        @pl.loop(chunks - 2, chunks)
        def _(k):
            send_part(k, far).wait_send()
            send_part(k, half).wait_send()

        cotan_copy(d, pair).wait_send()
        cotan_copy(other_d, pair).wait_send()

    @pl.when(inner)
    def _():
        def reduce_far(k):
            weight_wait(k)
            mine = partial(k, far)
            send_part(k, far).wait_recv()
            to_peer[k] = (mine + landed[k, far].astype(F32)).astype(BF16)
            send_peer(k).start()

        def reduce_half(k):
            mine = partial(k, half)
            send_part(k, half).wait_recv()
            own_sum[k] = mine + landed[k, half].astype(F32)

        def pointwise(k):
            @pl.when(k == 0)
            def _():
                own_cotan().wait()
                for row, depth in ((r, other_d), (pair, d), (pair, other_d)):
                    remote(
                        cotan_ref.at[:, pl.ds(0, width)],
                        cotan.at[aligned((row % 2) * block + depth * rows, rows), :],
                        cotan_send.at[0], cotan_recv.at[(row % 2) * 2 + depth],
                    ).wait_recv()

            send_peer(k).wait_recv()
            sums = own_sum[k] + from_peer[k].astype(F32)
            gate, up = sums[:, :LANES], sums[:, LANES:]
            cols = aligned(k * LANES, LANES)
            cot = cotan[:, cols].astype(F32)
            sigmoid = jax.nn.sigmoid(gate)
            silu = gate * sigmoid
            grads[k, half, :, pl.ds(0, LANES)] = (
                cot * up * sigmoid * (1.0 + gate * (1.0 - sigmoid))
            ).astype(BF16)
            grads[k, half, :, pl.ds(LANES, LANES)] = (cot * silu).astype(BF16)
            send_grads(k, half, peer, 0).start()
            send_grads(k, half, pair, 1).start()
            hidden_rows[:, cols] = (silu * up).astype(BF16)
            hidden_own[:, aligned(d * width + k * LANES, LANES)] = hidden_rows[
                aligned((r % 2) * block + d * rows, rows), cols
            ]

            @pl.when(k == chunks - 1)
            def _():
                send_hidden(0).start()

        def spread(k):
            send_grads(k, far, pair, 2).wait_recv()
            send_grads(k, far, pair, 2).start()

            @pl.when(k == chunks - 1)
            def _():
                send_hidden(1).start()
                send_hidden(2).start()

        @pl.loop(0, chunks + 2)
        def _(i):
            @pl.when(i < chunks)
            def _():
                reduce_far(i)

            @pl.when((i >= 1) & (i <= chunks))
            def _():
                pointwise(i - 1)

            @pl.when(i >= 2)
            def _():
                spread(i - 2)

            @pl.when(i < chunks)
            def _():
                reduce_half(i)

            @pl.when(i >= 2)
            def _():
                add_tokens_grad(i - 2)

        cotan_copy(other_d, r).wait_send()

    part[...] = total[...].astype(BF16)

    def core_copy(slot):
        col = (core, (core + 2) % 4)[slot]
        return remote(
            part.at[aligned(col * block, block), :], core_in.at[slot],
            core_send.at[slot], core_recv.at[slot], col=core,
        )

    core_copy(1).start()
    core_copy(0).start()
    turned[...] = tok[...].T
    keep_tokens().start()

    def plane_copy(way):
        where = (
            dict(col=across, depth=other_d), dict(col=across), dict(depth=other_d)
        )[way]
        depth = (other_d, d, other_d)[way]
        slot = (1, 1, 0)[way]
        return remote(
            plane_out.at[slot, aligned(depth * rows, rows), :], plane_in.at[way],
            plane_send.at[way], plane_recv.at[way], **where,
        )

    core_copy(1).wait_recv()
    plane_out[1] = (
        total[aligned(across * block, block), :] + core_in[1].astype(F32)
    ).astype(BF16)
    plane_copy(0).start()
    plane_copy(1).start()
    core_copy(0).wait_recv()
    plane_out[0] = (
        total[aligned(c * block, block), :] + core_in[0].astype(F32)
    ).astype(BF16)
    plane_copy(2).start()

    @pl.when(outer)
    def _():
        hidden_arrived(d).wait_recv()

    hidden_arrived(other_d).wait_recv()
    hidden_ref[...] = hidden_own[...]

    @pl.when(c != r)
    def _():
        first_hop().wait_send()

    for row in range(4):
        @pl.when(is_root)
        def _():
            forward(0, row, d).wait_send()

        @pl.when(is_even)
        def _():
            forward(1, row, d).wait_send()
            forward(2, row, d).wait_send()
            forward(2, row, other_d).wait_send()

    @pl.when(inner)
    def _():
        @pl.loop(0, chunks)
        def _(k):
            send_peer(k).wait_send()
            send_grads(k, half, peer, 0).wait_send()
            send_grads(k, half, pair, 1).wait_send()
            send_grads(k, far, pair, 2).wait_send()

        for way in range(3):
            send_hidden(way).wait_send()

    keep_tokens().wait()
    pltpu.make_async_copy(grad_gate_ref, grad_gate_ref, out_sem.at[1]).wait()
    pltpu.make_async_copy(grad_up_ref, grad_up_ref, out_sem.at[2]).wait()
    core_copy(0).wait_send()
    core_copy(1).wait_send()
    own = plane_out[0, aligned(d * rows, rows), :].astype(F32)
    for way in range(3):
        plane_copy(way).wait_recv()
        own = own + plane_in[way].astype(F32)
    grad_tokens_ref[...] = own.astype(BF16)
    for way in range(3):
        plane_copy(way).wait_send()


def exchange(tokens, gate_weight, up_weight, grad_hidden):
    rows, feats = tokens.shape
    cols = gate_weight.shape[1]
    chunks = cols // (2 * LANES)
    every = 8 * rows
    group = every // 2
    dma = pltpu.SemaphoreType.DMA
    vmem = pl.BlockSpec(memory_space=pltpu.VMEM)
    hbm = pl.BlockSpec(memory_space=pl.ANY)
    scratch = [
        pltpu.VMEM((every, feats), BF16),
        pltpu.VMEM((feats, every), BF16),
        pltpu.VMEM((chunks, feats, 2 * LANES), BF16),
        pltpu.VMEM((chunks, 2, group, 2 * LANES), BF16),
        pltpu.VMEM((chunks, 2, group, 2 * LANES), BF16),
        pltpu.VMEM((chunks, group, 2 * LANES), BF16),
        pltpu.VMEM((chunks, group, 2 * LANES), BF16),
        pltpu.VMEM((chunks, group, 2 * LANES), F32),
        pltpu.VMEM((chunks, 2, group, 2 * LANES), BF16),
        pltpu.VMEM((group, cols // 2), BF16),
        pltpu.VMEM((group, cols // 2), BF16),
        pltpu.VMEM((rows, cols), BF16),
        pltpu.VMEM((every, feats), F32),
        pltpu.VMEM((every, feats), BF16),
        pltpu.VMEM((2, 2 * rows, feats), BF16),
        pltpu.VMEM((2, 2 * rows, feats), BF16),
        pltpu.VMEM((3, rows, feats), BF16),
        dma((2, chunks)),
        dma((4, 8)),
        dma((8,)),
        dma((2,)),
        dma((4,)),
        dma,
        dma,
        dma((chunks, 2)),
        dma((chunks, 2)),
        dma((chunks,)),
        dma((chunks,)),
        dma((3, chunks)),
        dma((chunks, 2)),
        dma((3,)),
        dma((2,)),
        dma((3,)),
        dma((2,)),
        dma((2,)),
        dma((3,)),
        dma((3,)),
    ]
    return pl.pallas_call(
        kernel,
        out_shape=(
            jax.ShapeDtypeStruct((rows, cols), BF16),
            jax.ShapeDtypeStruct((rows, feats), BF16),
            jax.ShapeDtypeStruct((feats, every), BF16),
            jax.ShapeDtypeStruct((every, cols // 2), BF16),
            jax.ShapeDtypeStruct((every, cols // 2), BF16),
        ),
        in_specs=[hbm, hbm, hbm, hbm],
        out_specs=(vmem, vmem, hbm, hbm, hbm),
        scratch_shapes=scratch,
        compiler_params=pltpu.CompilerParams(
            collective_id=0, has_side_effects=True, vmem_limit_bytes=60 * 2**20
        ),
        cost_estimate=pl.CostEstimate(
            flops=8 * every * feats * cols // 2, bytes_accessed=4 * feats * cols,
            transcendentals=group * cols // 2,
        ),
    )(tokens, gate_weight, up_weight, grad_hidden)


def weight_kernel(tokens_ref, gate_ref, up_ref, gate_out, up_out, made, sem):
    cols = gate_ref.shape[1]
    steps, step = made.shape[1:3]
    width = 2 * LANES if cols % (2 * LANES) == 0 else LANES
    pairs = ((gate_ref, gate_out), (up_ref, up_out))

    def leave(at, which):
        return pltpu.make_async_copy(
            made.at[which, at], pairs[which][1].at[pl.ds(at * step, step), :], sem.at[which, at]
        )

    for at in range(steps):
        tokens = tokens_ref[pl.ds(at * step, step), :]
        for which in range(2):
            for col in range(0, cols, width):
                made[which, at, :, pl.ds(col, width)] = jnp.dot(
                    tokens, pairs[which][0][:, pl.ds(col, width)], preferred_element_type=F32
                )
            leave(at, which).start()
    for at in range(steps):
        for which in range(2):
            leave(at, which).wait()


def weight_grads(turned_tokens, grad_gate, grad_up):
    feats, every = turned_tokens.shape
    cols = grad_gate.shape[1]
    steps = 4
    shape = jax.ShapeDtypeStruct((feats, cols), F32)
    vmem = pl.BlockSpec(memory_space=pltpu.VMEM)
    hbm = pl.BlockSpec(memory_space=pl.ANY)
    return pl.pallas_call(
        weight_kernel,
        out_shape=(shape, shape),
        in_specs=[vmem, vmem, vmem],
        out_specs=(hbm, hbm),
        scratch_shapes=[
            pltpu.VMEM((2, steps, feats // steps, cols), F32),
            pltpu.SemaphoreType.DMA((2, steps)),
        ],
        compiler_params=pltpu.CompilerParams(vmem_limit_bytes=28 * 2**20),
        cost_estimate=pl.CostEstimate(
            flops=4 * every * feats * cols, bytes_accessed=8 * feats * cols, transcendentals=0
        ),
    )(turned_tokens, grad_gate, grad_up)


def on_line(tokens, gate_weight, up_weight, grad_hidden):
    hidden, grad_tokens, turned_tokens, grad_gate, grad_up = exchange(
        tokens, gate_weight, up_weight, grad_hidden
    )
    return (hidden, grad_tokens, *weight_grads(turned_tokens, grad_gate, grad_up))


def from_root(value, axis, source):
    kept = jnp.where(lax.axis_index(axis) == source, value, 0).astype(value.dtype)
    return lax.psum(kept, axis)


def local_grads(gate_pre, up_pre, cotangent):
    sigmoid_gate = jax.nn.sigmoid(gate_pre)
    cotan_f32 = cotangent.astype(jnp.float32)
    grad_gate = (
        cotan_f32 * up_pre * sigmoid_gate * (1.0 + gate_pre * (1.0 - sigmoid_gate))
    ).astype(jnp.bfloat16)
    grad_up = (cotan_f32 * jax.nn.silu(gate_pre)).astype(jnp.bfloat16)
    return (grad_gate, grad_up)


def matmul_f32(left, right):
    return jnp.dot(left, right, preferred_element_type=jnp.float32)


def rounded_term(left, right):
    return matmul_f32(left, right).astype(jnp.bfloat16).astype(jnp.float32)


def local(tokens, gate_weight, up_weight, grad_hidden):
    hidden_cols = gate_weight.shape[1]
    row_tokens = lax.all_gather(tokens, "row", axis=0, tiled=True)
    diag_panel = from_root(row_tokens, "col", lax.axis_index("row"))
    summed = lax.psum_scatter(
        jnp.concatenate(
            [rounded_term(diag_panel, gate_weight), rounded_term(diag_panel, up_weight)], 1
        ).astype(jnp.bfloat16),
        "row",
        scatter_dimension=0,
        tiled=True,
    ).astype(jnp.float32)
    gate_sum = summed[:, :hidden_cols]
    up_sum = summed[:, hidden_cols:]
    hidden = (jax.nn.silu(gate_sum) * up_sum).astype(jnp.bfloat16)
    own_gate, own_up = local_grads(gate_sum, up_sum, grad_hidden)
    grad_gate, grad_up = (
        lax.all_gather(own_gate, "row", axis=0, tiled=True),
        lax.all_gather(own_up, "row", axis=0, tiled=True),
    )
    first_term = jnp.einsum("tf,df->td", grad_gate, gate_weight, preferred_element_type=jnp.float32)
    grad_tokens = lax.psum_scatter(
        (
            first_term
            + jnp.einsum("tf,df->td", grad_up, up_weight, preferred_element_type=jnp.float32)
        ).astype(jnp.bfloat16),
        "col",
        scatter_dimension=0,
        tiled=True,
    )
    gate_slices, up_slices = (
        lax.all_to_all(grad_gate, "depth", split_axis=1, concat_axis=0, tiled=True),
        lax.all_to_all(grad_up, "depth", split_axis=1, concat_axis=0, tiled=True),
    )
    every_tokens = lax.all_gather(diag_panel, "depth", axis=0, tiled=True)
    grad_gate_weight = jnp.einsum(
        "td,tf->df", every_tokens, gate_slices, preferred_element_type=jnp.float32
    )
    grad_up_weight = jnp.einsum(
        "td,tf->df", every_tokens, up_slices, preferred_element_type=jnp.float32
    )
    return (hidden, grad_tokens, grad_gate_weight, grad_up_weight)


def pick(mesh, tokens, gate_weight, up_weight, grad_hidden):
    sizes = dict(mesh.shape)
    fits = (
        (sizes["row"], sizes["col"], sizes["depth"]) == (4, 4, 2)
        and tokens.shape[0] % 16 == 0
        and tokens.shape[1] % 128 == 0
        and gate_weight.shape[1] % (2 * LANES) == 0
    )
    plan = on_line if fits else local
    return plan(tokens, gate_weight, up_weight, grad_hidden)


def solution(mesh):
    return jax.shard_map(
        functools.partial(pick, mesh),
        mesh=mesh,
        in_specs=(
            P(("row", "depth"), "col"),
            P("row", "col"),
            P("row", "col"),
            P(("row", "depth"), "col"),
        ),
        out_specs=(
            P(("row", "depth"), "col"),
            P(("col", "depth"), "row"),
            P("row", ("col", "depth")),
            P("row", ("col", "depth")),
        ),
        check_vma=False,
    )
```

```python
import functools

import jax
import jax.numpy as jnp
from jax import lax
from jax.experimental import pallas as pl
from jax.experimental.pallas import tpu as pltpu
from jax.sharding import PartitionSpec as P

MESH = pl.DeviceIdType.MESH
LANES = 128
F32 = jnp.float32
BF16 = jnp.bfloat16


def aligned(start, size):
    return pl.ds(pl.multiple_of(start, size), size)


def kernel(
    tokens_ref, gate_ref, up_ref, cotan_ref,
    hidden_ref, grad_tokens_ref, every_tokens_ref, grads_ref,
    tok, turned, weights, sent, landed, to_peer, from_peer, own_sum, mine, grads, cotan, hidden_rows,
    hidden_own, total, part, core_in, plane_out, plane_in,
    w_sem, tok_send, tok_recv, cotan_send, cotan_recv, cotan_local, own_sem, sent_send, landed_recv,
    peer_send, peer_recv, grads_send, grads_recv, hidden_send, hidden_recv, out_sem,
    core_send, core_recv, plane_send, plane_recv,
):
    r, c, d = lax.axis_index("row"), lax.axis_index("col"), lax.axis_index("depth")
    other_d = 1 - d
    core = c + 1 - 2 * (c % 2)
    across = (c + 2) % 4
    pair = r + 1 - 2 * (r % 2)
    peer = 3 - r
    half = r // 2
    far = 1 - half
    chunks = weights.shape[0]
    width = chunks * LANES
    rows = tokens_ref.shape[0]
    block = 2 * rows
    group = 4 * rows

    def remote(src, dst, send, recv, **where):
        return pltpu.make_async_remote_copy(
            src_ref=src, dst_ref=dst, send_sem=send, recv_sem=recv,
            device_id={"row": r, "col": c, "depth": d, **where}, device_id_type=MESH,
        )

    def load(k, which):
        ref = (gate_ref, up_ref)[which]
        return pltpu.make_async_copy(
            ref.at[:, aligned(d * width + k * LANES, LANES)],
            weights.at[k, :, pl.ds(which * LANES, LANES)],
            w_sem.at[which, k],
        )

    @pl.loop(0, chunks)
    def _(k):
        load(k, 0).start()
        load(k, 1).start()

    barrier = pltpu.get_barrier_semaphore()
    partners = [dict(row=(r + step) % 4) for step in (1, 2, 3)] + [
        dict(row=pair, depth=other_d),
        dict(col=core),
        dict(col=across),
        dict(depth=other_d),
        dict(col=across, depth=other_d),
    ]
    for where in partners:
        pl.semaphore_signal(
            barrier, inc=1, device_id={"row": r, "col": c, "depth": d, **where},
            device_id_type=MESH,
        )
    pl.semaphore_wait(barrier, len(partners))

    def piece(row, depth):
        return tok.at[aligned(row * block + depth * rows, rows), :]

    is_root = c == r
    is_relay = across == r
    is_even = (c - r + 4) % 2 == 0

    def first_hop():
        return remote(
            tokens_ref, piece(r, d), tok_send.at[3, r * 2 + d], tok_recv.at[r * 2 + d], row=c
        )

    def forward(way, row, depth):
        where = (dict(col=across), dict(depth=other_d), dict(col=core))[way]
        at = row * 2 + depth
        return remote(
            piece(row, depth), piece(row, depth), tok_send.at[way, at], tok_recv.at[at], **where
        )

    def cotan_copy(depth, row):
        return remote(
            cotan_ref.at[:, aligned(depth * width, width)],
            cotan.at[aligned((r % 2) * block + d * rows, rows), :],
            cotan_send.at[depth], cotan_recv.at[(r % 2) * 2 + d], row=row, depth=depth,
        )

    def own_cotan():
        return pltpu.make_async_copy(
            cotan_ref.at[:, aligned(d * width, width)],
            cotan.at[aligned((r % 2) * block + d * rows, rows), :],
            cotan_local,
        )

    outer = (r == 0) | (r == 3)
    inner = (r == 1) | (r == 2)

    def own_tokens():
        return pltpu.make_async_copy(tokens_ref, piece(r, d), own_sem)

    @pl.when(c != r)
    def _():
        first_hop().start()

    @pl.when(is_root)
    def _():
        own_tokens().start()
        own_tokens().wait()

    order = (r, pair, 3 - pair, peer)

    def near(step):
        row = order[step]

        def arrive():
            forward(0, row, d).wait_recv()

        if step == 0:
            pl.when(c != r)(arrive)
        else:
            arrive()

        @pl.when(is_root)
        def _():
            forward(0, row, d).start()

        @pl.when(is_even)
        def _():
            forward(1, row, d).start()
            forward(2, row, d).start()

    def away(step):
        row = order[step]
        forward(1, row, other_d).wait_recv()

        @pl.when(is_even)
        def _():
            forward(2, row, other_d).start()

    def partial(k, which):
        return jnp.dot(
            tok[aligned(which * group, group), :], weights[k], preferred_element_type=F32
        )

    def partials(k):
        both = jnp.dot(tok[...], weights[k], preferred_element_type=F32)
        return both.reshape(2, group, 2 * LANES)

    def weight_wait(k):
        load(k, 0).wait()
        load(k, 1).wait()

    def send_part(k, which):
        return remote(
            sent.at[k, which], landed.at[k, which], sent_send.at[k, which],
            landed_recv.at[k, which], row=pair,
        )

    near(0)
    near(1)

    @pl.when(outer)
    def _():
        cotan_copy(d, pair).start()
        cotan_copy(other_d, pair).start()

    @pl.when(inner)
    def _():
        own_cotan().start()
        cotan_copy(other_d, r).start()

    away(0)
    away(1)

    @pl.when(outer)
    def _():
        weight_wait(0)
        sent[0, half] = partial(0, half).astype(BF16)
        send_part(0, half).start()

    near(2)
    away(2)
    near(3)
    away(3)

    def keep_tokens():
        return pltpu.make_async_copy(turned, every_tokens_ref, out_sem.at[0])

    def keep(k):
        return pltpu.make_async_copy(grads.at[k], grads_ref.at[k], out_sem.at[1])

    def add_tokens_grad(k):
        keep(k).start()

        @pl.when(k % 2 == 1)
        def _():
            step = min(256, total.shape[1])
            for at in range(0, total.shape[1], step):
                term = jnp.zeros((2 * group, step), F32)
                for chunk in (k - 1, k):
                    term += lax.dot_general(
                        grads[chunk].reshape(2 * group, 2 * LANES),
                        weights[chunk, pl.ds(at, step), :],
                        (((1,), (1,)), ((), ())), preferred_element_type=F32,
                    )
                total[:, pl.ds(at, step)] += term

    total[...] = jnp.zeros_like(total)

    def send_peer(k):
        return remote(to_peer.at[k], from_peer.at[k], peer_send.at[k], peer_recv.at[k], row=peer)

    def send_grads(k, which, to, way):
        return remote(
            grads.at[k, which], grads.at[k, which], grads_send.at[way, k],
            grads_recv.at[k, which], row=to,
        )

    def send_hidden(way):
        row, depth = ((r, other_d), (pair, d), (pair, other_d))[way]
        return remote(
            hidden_rows.at[aligned((row % 2) * block + depth * rows, rows), :],
            hidden_own.at[:, aligned(d * width, width)],
            hidden_send.at[way], hidden_recv.at[d], row=row, depth=depth,
        )

    def hidden_arrived(depth):
        return remote(
            hidden_rows.at[pl.ds(0, rows), :], hidden_own.at[:, aligned(depth * width, width)],
            hidden_send.at[0], hidden_recv.at[depth],
        )

    def take_grads(k):
        send_grads(k, half, r, 0).wait_recv()
        send_grads(k, far, r, 0).wait_recv()
        add_tokens_grad(k)

    lag = min(6, chunks)

    @pl.when(outer)
    def _():
        @pl.loop(0, chunks)
        def _(k):
            @pl.when(k >= 1)
            def _():
                weight_wait(k)

            @pl.when(k >= 2)
            def _():
                send_part(k - 2, far).wait_send()
                send_part(k - 2, half).wait_send()

            @pl.when(k == 0)
            def _():
                sent[k, far] = partial(k, far).astype(BF16)
                send_part(k, far).start()

            @pl.when(k >= 1)
            def _():
                sent[k] = partials(k).astype(BF16)
                send_part(k, far).start()
                send_part(k, half).start()

            @pl.when(k >= lag)
            def _():
                take_grads(k - lag)

        @pl.loop(chunks - lag, chunks)
        def _(k):
            take_grads(k)

        @pl.loop(chunks - 2, chunks)
        def _(k):
            send_part(k, far).wait_send()
            send_part(k, half).wait_send()

        cotan_copy(d, pair).wait_send()
        cotan_copy(other_d, pair).wait_send()

    @pl.when(inner)
    def _():
        def prepare(k):
            weight_wait(k)
            mine[...] = partials(k)

        def reduce_far(k):
            send_part(k, far).wait_recv()
            to_peer[k] = (mine[far] + landed[k, far].astype(F32)).astype(BF16)
            send_peer(k).start()

        def reduce_half(k):
            send_part(k, half).wait_recv()
            own_sum[k] = mine[half] + landed[k, half].astype(F32)

            @pl.when(k + 1 < chunks)
            def _():
                prepare(k + 1)

        def pointwise(k):
            @pl.when(k == 0)
            def _():
                own_cotan().wait()
                for row, depth in ((r, other_d), (pair, d), (pair, other_d)):
                    remote(
                        cotan_ref.at[:, pl.ds(0, width)],
                        cotan.at[aligned((row % 2) * block + depth * rows, rows), :],
                        cotan_send.at[0], cotan_recv.at[(row % 2) * 2 + depth],
                    ).wait_recv()

            send_peer(k).wait_recv()
            sums = own_sum[k] + from_peer[k].astype(F32)
            gate, up = sums[:, :LANES], sums[:, LANES:]
            cols = aligned(k * LANES, LANES)
            cot = cotan[:, cols].astype(F32)
            sigmoid = jax.nn.sigmoid(gate)
            silu = gate * sigmoid
            grads[k, half, :, pl.ds(0, LANES)] = (
                cot * up * sigmoid * (1.0 + gate * (1.0 - sigmoid))
            ).astype(BF16)
            grads[k, half, :, pl.ds(LANES, LANES)] = (cot * silu).astype(BF16)
            send_grads(k, half, peer, 0).start()
            send_grads(k, half, pair, 1).start()
            hidden_rows[:, cols] = (silu * up).astype(BF16)
            hidden_own[:, aligned(d * width + k * LANES, LANES)] = hidden_rows[
                aligned((r % 2) * block + d * rows, rows), cols
            ]

            @pl.when(k == chunks - 1)
            def _():
                send_hidden(0).start()

        def spread(k):
            send_grads(k, far, pair, 2).wait_recv()
            send_grads(k, far, pair, 2).start()

            @pl.when(k == chunks - 1)
            def _():
                send_hidden(1).start()
                send_hidden(2).start()

        prepare(0)

        @pl.loop(0, chunks + 2)
        def _(i):
            @pl.when(i < chunks)
            def _():
                reduce_far(i)

            @pl.when((i >= 1) & (i <= chunks))
            def _():
                pointwise(i - 1)

            @pl.when(i >= 2)
            def _():
                spread(i - 2)

            @pl.when(i < chunks)
            def _():
                reduce_half(i)

            @pl.when(i >= 2)
            def _():
                add_tokens_grad(i - 2)

        cotan_copy(other_d, r).wait_send()

    part[...] = total[...].astype(BF16)

    def core_copy(slot):
        col = (core, (core + 2) % 4)[slot]
        return remote(
            part.at[aligned(col * block, block), :], core_in.at[slot],
            core_send.at[slot], core_recv.at[slot], col=core,
        )

    core_copy(1).start()
    core_copy(0).start()
    turned[...] = tok[...].T
    keep_tokens().start()

    def plane_copy(way):
        where = (
            dict(col=across, depth=other_d), dict(col=across), dict(depth=other_d)
        )[way]
        depth = (other_d, d, other_d)[way]
        slot = (1, 1, 0)[way]
        return remote(
            plane_out.at[slot, aligned(depth * rows, rows), :], plane_in.at[way],
            plane_send.at[way], plane_recv.at[way], **where,
        )

    core_copy(1).wait_recv()
    plane_out[1] = (
        total[aligned(across * block, block), :] + core_in[1].astype(F32)
    ).astype(BF16)
    plane_copy(0).start()
    plane_copy(1).start()
    core_copy(0).wait_recv()
    plane_out[0] = (
        total[aligned(c * block, block), :] + core_in[0].astype(F32)
    ).astype(BF16)
    plane_copy(2).start()

    @pl.when(outer)
    def _():
        hidden_arrived(d).wait_recv()

    hidden_arrived(other_d).wait_recv()
    hidden_ref[...] = hidden_own[...]

    @pl.when(c != r)
    def _():
        first_hop().wait_send()

    for row in range(4):
        @pl.when(is_root)
        def _():
            forward(0, row, d).wait_send()

        @pl.when(is_even)
        def _():
            forward(1, row, d).wait_send()
            forward(2, row, d).wait_send()
            forward(2, row, other_d).wait_send()

    @pl.when(inner)
    def _():
        @pl.loop(0, chunks)
        def _(k):
            send_peer(k).wait_send()
            send_grads(k, half, peer, 0).wait_send()
            send_grads(k, half, pair, 1).wait_send()
            send_grads(k, far, pair, 2).wait_send()

        for way in range(3):
            send_hidden(way).wait_send()

    keep_tokens().wait()
    pltpu.make_async_copy(grads, grads_ref, out_sem.at[1]).wait()
    core_copy(0).wait_send()
    core_copy(1).wait_send()
    own = plane_out[0, aligned(d * rows, rows), :].astype(F32)
    for way in range(3):
        plane_copy(way).wait_recv()
        own = own + plane_in[way].astype(F32)
    grad_tokens_ref[...] = own.astype(BF16)
    for way in range(3):
        plane_copy(way).wait_send()


def exchange(tokens, gate_weight, up_weight, grad_hidden):
    rows, feats = tokens.shape
    cols = gate_weight.shape[1]
    chunks = cols // (2 * LANES)
    every = 8 * rows
    group = every // 2
    dma = pltpu.SemaphoreType.DMA
    vmem = pl.BlockSpec(memory_space=pltpu.VMEM)
    hbm = pl.BlockSpec(memory_space=pl.ANY)
    scratch = [
        pltpu.VMEM((every, feats), BF16),
        pltpu.VMEM((feats, every), BF16),
        pltpu.VMEM((chunks, feats, 2 * LANES), BF16),
        pltpu.VMEM((chunks, 2, group, 2 * LANES), BF16),
        pltpu.VMEM((chunks, 2, group, 2 * LANES), BF16),
        pltpu.VMEM((chunks, group, 2 * LANES), BF16),
        pltpu.VMEM((chunks, group, 2 * LANES), BF16),
        pltpu.VMEM((chunks, group, 2 * LANES), F32),
        pltpu.VMEM((2, group, 2 * LANES), F32),
        pltpu.VMEM((chunks, 2, group, 2 * LANES), BF16),
        pltpu.VMEM((group, cols // 2), BF16),
        pltpu.VMEM((group, cols // 2), BF16),
        pltpu.VMEM((rows, cols), BF16),
        pltpu.VMEM((every, feats), F32),
        pltpu.VMEM((every, feats), BF16),
        pltpu.VMEM((2, 2 * rows, feats), BF16),
        pltpu.VMEM((2, 2 * rows, feats), BF16),
        pltpu.VMEM((3, rows, feats), BF16),
        dma((2, chunks)),
        dma((4, 8)),
        dma((8,)),
        dma((2,)),
        dma((4,)),
        dma,
        dma,
        dma((chunks, 2)),
        dma((chunks, 2)),
        dma((chunks,)),
        dma((chunks,)),
        dma((3, chunks)),
        dma((chunks, 2)),
        dma((3,)),
        dma((2,)),
        dma((2,)),
        dma((2,)),
        dma((2,)),
        dma((3,)),
        dma((3,)),
    ]
    return pl.pallas_call(
        kernel,
        out_shape=(
            jax.ShapeDtypeStruct((rows, cols), BF16),
            jax.ShapeDtypeStruct((rows, feats), BF16),
            jax.ShapeDtypeStruct((feats, every), BF16),
            jax.ShapeDtypeStruct((chunks, 2, group, 2 * LANES), BF16),
        ),
        in_specs=[hbm, hbm, hbm, hbm],
        out_specs=(vmem, vmem, hbm, hbm),
        scratch_shapes=scratch,
        compiler_params=pltpu.CompilerParams(
            collective_id=0, has_side_effects=True, vmem_limit_bytes=60 * 2**20
        ),
        cost_estimate=pl.CostEstimate(
            flops=8 * every * feats * cols // 2, bytes_accessed=4 * feats * cols,
            transcendentals=group * cols // 2,
        ),
    )(tokens, gate_weight, up_weight, grad_hidden)


def weight_kernel(
    tokens_ref, grads_ref, hidden_ref, grad_tokens_ref,
    hidden_out, grad_tokens_out, gate_out, up_out, made, sem, carry_sem,
):
    chunks = grads_ref.shape[0]
    steps, step = made.shape[1:3]
    outs = (gate_out, up_out)
    carried = (
        pltpu.make_async_copy(hidden_ref, hidden_out, carry_sem.at[0]),
        pltpu.make_async_copy(grad_tokens_ref, grad_tokens_out, carry_sem.at[1]),
    )

    def leave(at, which):
        return pltpu.make_async_copy(
            made.at[which, at], outs[which].at[pl.ds(at * step, step), :], sem.at[which, at]
        )

    for copy in carried:
        copy.start()
    for at in range(steps):
        tokens = tokens_ref[pl.ds(at * step, step), :]
        for k in range(chunks):
            both = jnp.dot(
                tokens, grads_ref[k].reshape(tokens.shape[1], 2 * LANES),
                preferred_element_type=F32,
            )
            made[0, at, :, pl.ds(k * LANES, LANES)] = both[:, :LANES]
            made[1, at, :, pl.ds(k * LANES, LANES)] = both[:, LANES:]
        leave(at, 0).start()
        leave(at, 1).start()
    for at in range(steps):
        leave(at, 0).wait()
        leave(at, 1).wait()
    for copy in carried:
        copy.wait()


def weight_grads(turned_tokens, grads, hidden, grad_tokens):
    feats, every = turned_tokens.shape
    cols = grads.shape[0] * LANES
    steps = 4
    shape = jax.ShapeDtypeStruct((feats, cols), F32)
    vmem = pl.BlockSpec(memory_space=pltpu.VMEM)
    hbm = pl.BlockSpec(memory_space=pl.ANY)
    return pl.pallas_call(
        weight_kernel,
        out_shape=(
            jax.ShapeDtypeStruct(hidden.shape, hidden.dtype),
            jax.ShapeDtypeStruct(grad_tokens.shape, grad_tokens.dtype),
            shape,
            shape,
        ),
        in_specs=[vmem, vmem, hbm, hbm],
        out_specs=(hbm, hbm, hbm, hbm),
        scratch_shapes=[
            pltpu.VMEM((2, steps, feats // steps, cols), F32),
            pltpu.SemaphoreType.DMA((2, steps)),
            pltpu.SemaphoreType.DMA((2,)),
        ],
        compiler_params=pltpu.CompilerParams(vmem_limit_bytes=60 * 2**20),
        cost_estimate=pl.CostEstimate(
            flops=4 * every * feats * cols, bytes_accessed=8 * feats * cols, transcendentals=0
        ),
    )(turned_tokens, grads, hidden, grad_tokens)


def on_line(tokens, gate_weight, up_weight, grad_hidden):
    hidden, grad_tokens, turned_tokens, grads = exchange(
        tokens, gate_weight, up_weight, grad_hidden
    )
    return weight_grads(turned_tokens, grads, hidden, grad_tokens)


def from_root(value, axis, source):
    kept = jnp.where(lax.axis_index(axis) == source, value, 0).astype(value.dtype)
    return lax.psum(kept, axis)


def local_grads(gate_pre, up_pre, cotangent):
    sigmoid_gate = jax.nn.sigmoid(gate_pre)
    cotan_f32 = cotangent.astype(jnp.float32)
    grad_gate = (
        cotan_f32 * up_pre * sigmoid_gate * (1.0 + gate_pre * (1.0 - sigmoid_gate))
    ).astype(jnp.bfloat16)
    grad_up = (cotan_f32 * jax.nn.silu(gate_pre)).astype(jnp.bfloat16)
    return (grad_gate, grad_up)


def matmul_f32(left, right):
    return jnp.dot(left, right, preferred_element_type=jnp.float32)


def rounded_term(left, right):
    return matmul_f32(left, right).astype(jnp.bfloat16).astype(jnp.float32)


def local(tokens, gate_weight, up_weight, grad_hidden):
    hidden_cols = gate_weight.shape[1]
    row_tokens = lax.all_gather(tokens, "row", axis=0, tiled=True)
    diag_panel = from_root(row_tokens, "col", lax.axis_index("row"))
    summed = lax.psum_scatter(
        jnp.concatenate(
            [rounded_term(diag_panel, gate_weight), rounded_term(diag_panel, up_weight)], 1
        ).astype(jnp.bfloat16),
        "row",
        scatter_dimension=0,
        tiled=True,
    ).astype(jnp.float32)
    gate_sum = summed[:, :hidden_cols]
    up_sum = summed[:, hidden_cols:]
    hidden = (jax.nn.silu(gate_sum) * up_sum).astype(jnp.bfloat16)
    own_gate, own_up = local_grads(gate_sum, up_sum, grad_hidden)
    grad_gate, grad_up = (
        lax.all_gather(own_gate, "row", axis=0, tiled=True),
        lax.all_gather(own_up, "row", axis=0, tiled=True),
    )
    first_term = jnp.einsum("tf,df->td", grad_gate, gate_weight, preferred_element_type=jnp.float32)
    grad_tokens = lax.psum_scatter(
        (
            first_term
            + jnp.einsum("tf,df->td", grad_up, up_weight, preferred_element_type=jnp.float32)
        ).astype(jnp.bfloat16),
        "col",
        scatter_dimension=0,
        tiled=True,
    )
    gate_slices, up_slices = (
        lax.all_to_all(grad_gate, "depth", split_axis=1, concat_axis=0, tiled=True),
        lax.all_to_all(grad_up, "depth", split_axis=1, concat_axis=0, tiled=True),
    )
    every_tokens = lax.all_gather(diag_panel, "depth", axis=0, tiled=True)
    grad_gate_weight = jnp.einsum(
        "td,tf->df", every_tokens, gate_slices, preferred_element_type=jnp.float32
    )
    grad_up_weight = jnp.einsum(
        "td,tf->df", every_tokens, up_slices, preferred_element_type=jnp.float32
    )
    return (hidden, grad_tokens, grad_gate_weight, grad_up_weight)


def pick(mesh, tokens, gate_weight, up_weight, grad_hidden):
    sizes = dict(mesh.shape)
    fits = (
        (sizes["row"], sizes["col"], sizes["depth"]) == (4, 4, 2)
        and tokens.shape[0] % 16 == 0
        and tokens.shape[1] % 128 == 0
        and gate_weight.shape[1] % (4 * LANES) == 0
    )
    plan = on_line if fits else local
    return plan(tokens, gate_weight, up_weight, grad_hidden)


def solution(mesh):
    return jax.shard_map(
        functools.partial(pick, mesh),
        mesh=mesh,
        in_specs=(
            P(("row", "depth"), "col"),
            P("row", "col"),
            P("row", "col"),
            P(("row", "depth"), "col"),
        ),
        out_specs=(
            P(("row", "depth"), "col"),
            P(("col", "depth"), "row"),
            P("row", ("col", "depth")),
            P("row", ("col", "depth")),
        ),
        check_vma=False,
    )
```

```python
import functools

import jax
import jax.numpy as jnp
from jax import lax
from jax.experimental import pallas as pl
from jax.experimental.pallas import tpu as pltpu
from jax.sharding import PartitionSpec as P

MESH = pl.DeviceIdType.MESH
LANES = 128
F32 = jnp.float32
BF16 = jnp.bfloat16


def aligned(start, size):
    return pl.ds(pl.multiple_of(start, size), size)


def kernel(
    tokens_ref, gate_ref, up_ref, cotan_ref,
    hidden_ref, grad_tokens_ref, every_tokens_ref, grads_ref,
    tok, turned, weights, sent, landed, to_peer, from_peer, own_sum, mine, grads, cotan, hidden_rows,
    hidden_own, total, part, core_in, plane_out, plane_in,
    w_sem, tok_send, tok_recv, cotan_send, cotan_recv, cotan_local, own_sem, sent_send, landed_recv,
    peer_send, peer_recv, grads_send, grads_recv, hidden_send, hidden_recv, out_sem,
    core_send, core_recv, plane_send, plane_recv,
):
    r, c, d = lax.axis_index("row"), lax.axis_index("col"), lax.axis_index("depth")
    other_d = 1 - d
    core = c + 1 - 2 * (c % 2)
    across = (c + 2) % 4
    pair = r + 1 - 2 * (r % 2)
    peer = 3 - r
    half = r // 2
    far = 1 - half
    chunks = weights.shape[0]
    width = chunks * LANES
    rows = tokens_ref.shape[0]
    block = 2 * rows
    group = 4 * rows

    def remote(src, dst, send, recv, **where):
        return pltpu.make_async_remote_copy(
            src_ref=src, dst_ref=dst, send_sem=send, recv_sem=recv,
            device_id={"row": r, "col": c, "depth": d, **where}, device_id_type=MESH,
        )

    def load(k, which):
        ref = (gate_ref, up_ref)[which]
        return pltpu.make_async_copy(
            ref.at[:, aligned(d * width + k * LANES, LANES)],
            weights.at[k, :, pl.ds(which * LANES, LANES)],
            w_sem.at[which, k],
        )

    @pl.loop(0, chunks)
    def _(k):
        load(k, 0).start()
        load(k, 1).start()

    barrier = pltpu.get_barrier_semaphore()
    partners = [dict(row=(r + step) % 4) for step in (1, 2, 3)] + [
        dict(row=pair, depth=other_d),
        dict(col=core),
        dict(col=across),
        dict(depth=other_d),
        dict(col=across, depth=other_d),
    ]
    for where in partners:
        pl.semaphore_signal(
            barrier, inc=1, device_id={"row": r, "col": c, "depth": d, **where},
            device_id_type=MESH,
        )
    pl.semaphore_wait(barrier, len(partners))

    def piece(row, depth):
        return tok.at[aligned(row * block + depth * rows, rows), :]

    is_root = c == r
    is_relay = across == r
    is_even = (c - r + 4) % 2 == 0

    def first_hop():
        return remote(
            tokens_ref, piece(r, d), tok_send.at[3, r * 2 + d], tok_recv.at[r * 2 + d], row=c
        )

    def forward(way, row, depth):
        where = (dict(col=across), dict(depth=other_d), dict(col=core))[way]
        at = row * 2 + depth
        return remote(
            piece(row, depth), piece(row, depth), tok_send.at[way, at], tok_recv.at[at], **where
        )

    def cotan_copy(depth, row):
        return remote(
            cotan_ref.at[:, aligned(depth * width, width)],
            cotan.at[aligned((r % 2) * block + d * rows, rows), :],
            cotan_send.at[depth], cotan_recv.at[(r % 2) * 2 + d], row=row, depth=depth,
        )

    def own_cotan():
        return pltpu.make_async_copy(
            cotan_ref.at[:, aligned(d * width, width)],
            cotan.at[aligned((r % 2) * block + d * rows, rows), :],
            cotan_local,
        )

    outer = (r == 0) | (r == 3)
    inner = (r == 1) | (r == 2)

    def own_tokens():
        return pltpu.make_async_copy(tokens_ref, piece(r, d), own_sem)

    @pl.when(c != r)
    def _():
        first_hop().start()

    @pl.when(is_root)
    def _():
        own_tokens().start()
        own_tokens().wait()

    order = (r, pair, 3 - pair, peer)

    def near(step):
        row = order[step]

        def arrive():
            forward(0, row, d).wait_recv()

        if step == 0:
            pl.when(c != r)(arrive)
        else:
            arrive()

        @pl.when(is_root)
        def _():
            forward(0, row, d).start()

        @pl.when(is_even)
        def _():
            forward(1, row, d).start()
            forward(2, row, d).start()

    def away(step):
        row = order[step]
        forward(1, row, other_d).wait_recv()

        @pl.when(is_even)
        def _():
            forward(2, row, other_d).start()

    def partial(k, which):
        return jnp.dot(
            tok[aligned(which * group, group), :], weights[k], preferred_element_type=F32
        )

    def partials(k):
        both = jnp.dot(tok[...], weights[k], preferred_element_type=F32)
        return both.reshape(2, group, 2 * LANES)

    def weight_wait(k):
        load(k, 0).wait()
        load(k, 1).wait()

    def send_part(k, which):
        return remote(
            sent.at[k, which], landed.at[k, which], sent_send.at[k, which],
            landed_recv.at[k, which], row=pair,
        )

    near(0)
    near(1)

    @pl.when(outer)
    def _():
        cotan_copy(d, pair).start()
        cotan_copy(other_d, pair).start()

    @pl.when(inner)
    def _():
        own_cotan().start()
        cotan_copy(other_d, r).start()

    away(0)
    away(1)

    @pl.when(outer)
    def _():
        weight_wait(0)
        sent[0, half] = partial(0, half).astype(BF16)
        send_part(0, half).start()

    near(2)
    away(2)
    near(3)
    away(3)

    def keep_tokens():
        return pltpu.make_async_copy(turned, every_tokens_ref, out_sem.at[0])

    def keep(k):
        return pltpu.make_async_copy(grads.at[k], grads_ref.at[k], out_sem.at[1])

    def add_tokens_grad(k):
        keep(k).start()

        @pl.when(k % 2 == 1)
        def _():
            step = min(256, total.shape[1])
            for at in range(0, total.shape[1], step):
                term = jnp.zeros((2 * group, step), F32)
                for chunk in (k - 1, k):
                    term += lax.dot_general(
                        grads[chunk].reshape(2 * group, 2 * LANES),
                        weights[chunk, pl.ds(at, step), :],
                        (((1,), (1,)), ((), ())), preferred_element_type=F32,
                    )
                total[:, pl.ds(at, step)] += term

    total[...] = jnp.zeros_like(total)

    def send_peer(k):
        return remote(to_peer.at[k], from_peer.at[k], peer_send.at[k], peer_recv.at[k], row=peer)

    def send_grads(k, which, to, way):
        return remote(
            grads.at[k, which], grads.at[k, which], grads_send.at[way, k],
            grads_recv.at[k, which], row=to,
        )

    def send_hidden(way):
        row, depth = ((r, other_d), (pair, d), (pair, other_d))[way]
        return remote(
            hidden_rows.at[aligned((row % 2) * block + depth * rows, rows), :],
            hidden_own.at[:, aligned(d * width, width)],
            hidden_send.at[way], hidden_recv.at[d], row=row, depth=depth,
        )

    def hidden_arrived(depth):
        return remote(
            hidden_rows.at[pl.ds(0, rows), :], hidden_own.at[:, aligned(depth * width, width)],
            hidden_send.at[0], hidden_recv.at[depth],
        )

    def take_grads(k):
        send_grads(k, half, r, 0).wait_recv()
        send_grads(k, far, r, 0).wait_recv()
        add_tokens_grad(k)

    lag = min(12, chunks)
    flight = min(3, chunks)
    point_lag, spread_lag = 2, 4

    @pl.when(outer)
    def _():
        @pl.loop(0, chunks)
        def _(k):
            @pl.when(k >= 1)
            def _():
                weight_wait(k)

            @pl.when(k >= flight)
            def _():
                send_part(k - flight, far).wait_send()
                send_part(k - flight, half).wait_send()

            @pl.when(k == 0)
            def _():
                sent[k, far] = partial(k, far).astype(BF16)
                send_part(k, far).start()

            @pl.when(k >= 1)
            def _():
                sent[k] = partials(k).astype(BF16)
                send_part(k, far).start()
                send_part(k, half).start()

            @pl.when(k >= lag)
            def _():
                take_grads(k - lag)

        @pl.loop(chunks - lag, chunks)
        def _(k):
            take_grads(k)

        @pl.loop(chunks - flight, chunks)
        def _(k):
            send_part(k, far).wait_send()
            send_part(k, half).wait_send()

        cotan_copy(d, pair).wait_send()
        cotan_copy(other_d, pair).wait_send()

    @pl.when(inner)
    def _():
        def prepare(k):
            weight_wait(k)
            mine[...] = partials(k)

        def reduce_far(k):
            send_part(k, far).wait_recv()
            to_peer[k] = (mine[far] + landed[k, far].astype(F32)).astype(BF16)
            send_peer(k).start()

        def reduce_half(k):
            send_part(k, half).wait_recv()
            own_sum[k] = mine[half] + landed[k, half].astype(F32)

            @pl.when(k + 1 < chunks)
            def _():
                prepare(k + 1)

        def pointwise(k):
            @pl.when(k == 0)
            def _():
                own_cotan().wait()
                for row, depth in ((r, other_d), (pair, d), (pair, other_d)):
                    remote(
                        cotan_ref.at[:, pl.ds(0, width)],
                        cotan.at[aligned((row % 2) * block + depth * rows, rows), :],
                        cotan_send.at[0], cotan_recv.at[(row % 2) * 2 + depth],
                    ).wait_recv()

            send_peer(k).wait_recv()
            sums = own_sum[k] + from_peer[k].astype(F32)
            gate, up = sums[:, :LANES], sums[:, LANES:]
            cols = aligned(k * LANES, LANES)
            cot = cotan[:, cols].astype(F32)
            sigmoid = jax.nn.sigmoid(gate)
            silu = gate * sigmoid
            grads[k, half, :, pl.ds(0, LANES)] = (
                cot * up * sigmoid * (1.0 + gate * (1.0 - sigmoid))
            ).astype(BF16)
            grads[k, half, :, pl.ds(LANES, LANES)] = (cot * silu).astype(BF16)
            send_grads(k, half, peer, 0).start()
            send_grads(k, half, pair, 1).start()
            hidden_rows[:, cols] = (silu * up).astype(BF16)
            hidden_own[:, aligned(d * width + k * LANES, LANES)] = hidden_rows[
                aligned((r % 2) * block + d * rows, rows), cols
            ]

            @pl.when(k == chunks - 1)
            def _():
                send_hidden(0).start()

        def spread(k):
            send_grads(k, far, pair, 2).wait_recv()
            send_grads(k, far, pair, 2).start()

            @pl.when(k == chunks - 1)
            def _():
                send_hidden(1).start()
                send_hidden(2).start()

        prepare(0)

        @pl.loop(0, chunks + spread_lag)
        def _(i):
            @pl.when(i < chunks)
            def _():
                reduce_far(i)

            @pl.when((i >= point_lag) & (i < chunks + point_lag))
            def _():
                pointwise(i - point_lag)

            @pl.when(i < chunks)
            def _():
                reduce_half(i)

            @pl.when(i >= spread_lag)
            def _():
                spread(i - spread_lag)
                add_tokens_grad(i - spread_lag)

        cotan_copy(other_d, r).wait_send()

    part[...] = total[...].astype(BF16)

    def core_copy(slot):
        col = (core, (core + 2) % 4)[slot]
        return remote(
            part.at[aligned(col * block, block), :], core_in.at[slot],
            core_send.at[slot], core_recv.at[slot], col=core,
        )

    core_copy(1).start()
    core_copy(0).start()
    turned[...] = tok[...].T
    keep_tokens().start()

    def plane_copy(way):
        where = (
            dict(col=across, depth=other_d), dict(col=across), dict(depth=other_d)
        )[way]
        depth = (other_d, d, other_d)[way]
        slot = (1, 1, 0)[way]
        return remote(
            plane_out.at[slot, aligned(depth * rows, rows), :], plane_in.at[way],
            plane_send.at[way], plane_recv.at[way], **where,
        )

    core_copy(1).wait_recv()
    plane_out[1] = (
        total[aligned(across * block, block), :] + core_in[1].astype(F32)
    ).astype(BF16)
    plane_copy(0).start()
    plane_copy(1).start()
    core_copy(0).wait_recv()
    plane_out[0] = (
        total[aligned(c * block, block), :] + core_in[0].astype(F32)
    ).astype(BF16)
    plane_copy(2).start()

    @pl.when(outer)
    def _():
        hidden_arrived(d).wait_recv()

    hidden_arrived(other_d).wait_recv()
    hidden_ref[...] = hidden_own[...]

    @pl.when(c != r)
    def _():
        first_hop().wait_send()

    for row in range(4):
        @pl.when(is_root)
        def _():
            forward(0, row, d).wait_send()

        @pl.when(is_even)
        def _():
            forward(1, row, d).wait_send()
            forward(2, row, d).wait_send()
            forward(2, row, other_d).wait_send()

    @pl.when(inner)
    def _():
        @pl.loop(0, chunks)
        def _(k):
            send_peer(k).wait_send()
            send_grads(k, half, peer, 0).wait_send()
            send_grads(k, half, pair, 1).wait_send()
            send_grads(k, far, pair, 2).wait_send()

        for way in range(3):
            send_hidden(way).wait_send()

    keep_tokens().wait()
    pltpu.make_async_copy(grads, grads_ref, out_sem.at[1]).wait()
    core_copy(0).wait_send()
    core_copy(1).wait_send()
    own = plane_out[0, aligned(d * rows, rows), :].astype(F32)
    for way in range(3):
        plane_copy(way).wait_recv()
        own = own + plane_in[way].astype(F32)
    grad_tokens_ref[...] = own.astype(BF16)
    for way in range(3):
        plane_copy(way).wait_send()


def exchange(tokens, gate_weight, up_weight, grad_hidden):
    rows, feats = tokens.shape
    cols = gate_weight.shape[1]
    chunks = cols // (2 * LANES)
    every = 8 * rows
    group = every // 2
    dma = pltpu.SemaphoreType.DMA
    vmem = pl.BlockSpec(memory_space=pltpu.VMEM)
    hbm = pl.BlockSpec(memory_space=pl.ANY)
    scratch = [
        pltpu.VMEM((every, feats), BF16),
        pltpu.VMEM((feats, every), BF16),
        pltpu.VMEM((chunks, feats, 2 * LANES), BF16),
        pltpu.VMEM((chunks, 2, group, 2 * LANES), BF16),
        pltpu.VMEM((chunks, 2, group, 2 * LANES), BF16),
        pltpu.VMEM((chunks, group, 2 * LANES), BF16),
        pltpu.VMEM((chunks, group, 2 * LANES), BF16),
        pltpu.VMEM((chunks, group, 2 * LANES), F32),
        pltpu.VMEM((2, group, 2 * LANES), F32),
        pltpu.VMEM((chunks, 2, group, 2 * LANES), BF16),
        pltpu.VMEM((group, cols // 2), BF16),
        pltpu.VMEM((group, cols // 2), BF16),
        pltpu.VMEM((rows, cols), BF16),
        pltpu.VMEM((every, feats), F32),
        pltpu.VMEM((every, feats), BF16),
        pltpu.VMEM((2, 2 * rows, feats), BF16),
        pltpu.VMEM((2, 2 * rows, feats), BF16),
        pltpu.VMEM((3, rows, feats), BF16),
        dma((2, chunks)),
        dma((4, 8)),
        dma((8,)),
        dma((2,)),
        dma((4,)),
        dma,
        dma,
        dma((chunks, 2)),
        dma((chunks, 2)),
        dma((chunks,)),
        dma((chunks,)),
        dma((3, chunks)),
        dma((chunks, 2)),
        dma((3,)),
        dma((2,)),
        dma((2,)),
        dma((2,)),
        dma((2,)),
        dma((3,)),
        dma((3,)),
    ]
    return pl.pallas_call(
        kernel,
        out_shape=(
            jax.ShapeDtypeStruct((rows, cols), BF16),
            jax.ShapeDtypeStruct((rows, feats), BF16),
            jax.ShapeDtypeStruct((feats, every), BF16),
            jax.ShapeDtypeStruct((chunks, 2, group, 2 * LANES), BF16),
        ),
        in_specs=[hbm, hbm, hbm, hbm],
        out_specs=(vmem, vmem, hbm, hbm),
        scratch_shapes=scratch,
        compiler_params=pltpu.CompilerParams(
            collective_id=0, has_side_effects=True, vmem_limit_bytes=60 * 2**20
        ),
        cost_estimate=pl.CostEstimate(
            flops=8 * every * feats * cols // 2, bytes_accessed=4 * feats * cols,
            transcendentals=group * cols // 2,
        ),
    )(tokens, gate_weight, up_weight, grad_hidden)


def weight_kernel(
    tokens_ref, grads_ref, hidden_ref, grad_tokens_ref,
    hidden_out, grad_tokens_out, gate_out, up_out,
    tokens, grads, hidden, grad_tokens, made, sem, load_sem, grads_sem, carry_sem,
):
    chunks = grads_ref.shape[0]
    steps, step = made.shape[1:3]
    part = step // 2
    outs = (gate_out, up_out)
    carried = (
        (hidden_ref, hidden, hidden_out),
        (grad_tokens_ref, grad_tokens, grad_tokens_out),
    )

    def load_tokens(at):
        rows = pl.ds(at * step, step)
        return pltpu.make_async_copy(
            tokens_ref.at[rows, :], tokens.at[rows, :], load_sem.at[at]
        )

    def load_grads(k):
        return pltpu.make_async_copy(grads_ref.at[k], grads.at[k], grads_sem.at[k])

    def carry(which, way):
        return pltpu.make_async_copy(
            carried[which][way], carried[which][way + 1], carry_sem.at[way, which]
        )

    def leave(at, which, piece):
        return pltpu.make_async_copy(
            made.at[which, at, pl.ds(piece * part, part), :],
            outs[which].at[pl.ds(at * step + piece * part, part), :],
            sem.at[which, at, piece],
        )

    load_tokens(0).start()
    for k in range(chunks):
        load_grads(k).start()
    for at in range(1, steps):
        load_tokens(at).start()
    for which in range(2):
        carry(which, 0).start()
    for at in range(steps):
        load_tokens(at).wait()
        left = tokens[pl.ds(at * step, step), :]
        for k in range(chunks):
            if at == 0:
                load_grads(k).wait()
            both = jnp.dot(
                left, grads[k].reshape(left.shape[1], 2 * LANES), preferred_element_type=F32
            )
            made[0, at, :, pl.ds(k * LANES, LANES)] = both[:, :LANES]
            made[1, at, :, pl.ds(k * LANES, LANES)] = both[:, LANES:]
        for which in range(2):
            for piece in range(2):
                leave(at, which, piece).start()
        if at == 0:
            for which in range(2):
                carry(which, 0).wait()
                carry(which, 1).start()
    for at in range(steps):
        for which in range(2):
            for piece in range(2):
                leave(at, which, piece).wait()
    for which in range(2):
        carry(which, 1).wait()


def weight_grads(turned_tokens, grads, hidden, grad_tokens):
    feats, every = turned_tokens.shape
    cols = grads.shape[0] * LANES
    steps = 4
    shape = jax.ShapeDtypeStruct((feats, cols), F32)
    hbm = pl.BlockSpec(memory_space=pl.ANY)
    return pl.pallas_call(
        weight_kernel,
        out_shape=(
            jax.ShapeDtypeStruct(hidden.shape, hidden.dtype),
            jax.ShapeDtypeStruct(grad_tokens.shape, grad_tokens.dtype),
            shape,
            shape,
        ),
        in_specs=[hbm, hbm, hbm, hbm],
        out_specs=(hbm, hbm, hbm, hbm),
        scratch_shapes=[
            pltpu.VMEM(turned_tokens.shape, BF16),
            pltpu.VMEM(grads.shape, BF16),
            pltpu.VMEM(hidden.shape, BF16),
            pltpu.VMEM(grad_tokens.shape, BF16),
            pltpu.VMEM((2, steps, feats // steps, cols), F32),
            pltpu.SemaphoreType.DMA((2, steps, 2)),
            pltpu.SemaphoreType.DMA((steps,)),
            pltpu.SemaphoreType.DMA((grads.shape[0],)),
            pltpu.SemaphoreType.DMA((2, 2)),
        ],
        compiler_params=pltpu.CompilerParams(vmem_limit_bytes=60 * 2**20),
        cost_estimate=pl.CostEstimate(
            flops=4 * every * feats * cols, bytes_accessed=8 * feats * cols, transcendentals=0
        ),
    )(turned_tokens, grads, hidden, grad_tokens)


def on_line(tokens, gate_weight, up_weight, grad_hidden):
    hidden, grad_tokens, turned_tokens, grads = exchange(
        tokens, gate_weight, up_weight, grad_hidden
    )
    return weight_grads(turned_tokens, grads, hidden, grad_tokens)


def from_root(value, axis, source):
    kept = jnp.where(lax.axis_index(axis) == source, value, 0).astype(value.dtype)
    return lax.psum(kept, axis)


def local_grads(gate_pre, up_pre, cotangent):
    sigmoid_gate = jax.nn.sigmoid(gate_pre)
    cotan_f32 = cotangent.astype(jnp.float32)
    grad_gate = (
        cotan_f32 * up_pre * sigmoid_gate * (1.0 + gate_pre * (1.0 - sigmoid_gate))
    ).astype(jnp.bfloat16)
    grad_up = (cotan_f32 * jax.nn.silu(gate_pre)).astype(jnp.bfloat16)
    return (grad_gate, grad_up)


def matmul_f32(left, right):
    return jnp.dot(left, right, preferred_element_type=jnp.float32)


def rounded_term(left, right):
    return matmul_f32(left, right).astype(jnp.bfloat16).astype(jnp.float32)


def local(tokens, gate_weight, up_weight, grad_hidden):
    hidden_cols = gate_weight.shape[1]
    row_tokens = lax.all_gather(tokens, "row", axis=0, tiled=True)
    diag_panel = from_root(row_tokens, "col", lax.axis_index("row"))
    summed = lax.psum_scatter(
        jnp.concatenate(
            [rounded_term(diag_panel, gate_weight), rounded_term(diag_panel, up_weight)], 1
        ).astype(jnp.bfloat16),
        "row",
        scatter_dimension=0,
        tiled=True,
    ).astype(jnp.float32)
    gate_sum = summed[:, :hidden_cols]
    up_sum = summed[:, hidden_cols:]
    hidden = (jax.nn.silu(gate_sum) * up_sum).astype(jnp.bfloat16)
    own_gate, own_up = local_grads(gate_sum, up_sum, grad_hidden)
    grad_gate, grad_up = (
        lax.all_gather(own_gate, "row", axis=0, tiled=True),
        lax.all_gather(own_up, "row", axis=0, tiled=True),
    )
    first_term = jnp.einsum("tf,df->td", grad_gate, gate_weight, preferred_element_type=jnp.float32)
    grad_tokens = lax.psum_scatter(
        (
            first_term
            + jnp.einsum("tf,df->td", grad_up, up_weight, preferred_element_type=jnp.float32)
        ).astype(jnp.bfloat16),
        "col",
        scatter_dimension=0,
        tiled=True,
    )
    gate_slices, up_slices = (
        lax.all_to_all(grad_gate, "depth", split_axis=1, concat_axis=0, tiled=True),
        lax.all_to_all(grad_up, "depth", split_axis=1, concat_axis=0, tiled=True),
    )
    every_tokens = lax.all_gather(diag_panel, "depth", axis=0, tiled=True)
    grad_gate_weight = jnp.einsum(
        "td,tf->df", every_tokens, gate_slices, preferred_element_type=jnp.float32
    )
    grad_up_weight = jnp.einsum(
        "td,tf->df", every_tokens, up_slices, preferred_element_type=jnp.float32
    )
    return (hidden, grad_tokens, grad_gate_weight, grad_up_weight)


def pick(mesh, tokens, gate_weight, up_weight, grad_hidden):
    sizes = dict(mesh.shape)
    fits = (
        (sizes["row"], sizes["col"], sizes["depth"]) == (4, 4, 2)
        and tokens.shape[0] % 16 == 0
        and tokens.shape[1] % 128 == 0
        and gate_weight.shape[1] % (4 * LANES) == 0
    )
    plan = on_line if fits else local
    return plan(tokens, gate_weight, up_weight, grad_hidden)


def solution(mesh):
    return jax.shard_map(
        functools.partial(pick, mesh),
        mesh=mesh,
        in_specs=(
            P(("row", "depth"), "col"),
            P("row", "col"),
            P("row", "col"),
            P(("row", "depth"), "col"),
        ),
        out_specs=(
            P(("row", "depth"), "col"),
            P(("col", "depth"), "row"),
            P("row", ("col", "depth")),
            P("row", ("col", "depth")),
        ),
        check_vma=False,
    )
```

```python
import functools

import jax
import jax.numpy as jnp
from jax import lax
from jax.experimental import pallas as pl
from jax.experimental.pallas import tpu as pltpu
from jax.sharding import PartitionSpec as P

MESH = pl.DeviceIdType.MESH
LANES = 128
F32 = jnp.float32
BF16 = jnp.bfloat16


def aligned(start, size):
    return pl.ds(pl.multiple_of(start, size), size)


def kernel(
    tokens_ref, gate_ref, up_ref, cotan_ref,
    hidden_ref, grad_tokens_ref, every_tokens_ref, grad_gate_ref, grad_up_ref,
    tok, turned, weights, sent, landed, to_peer, from_peer, own_sum, mine, grads, cotan, hidden_rows,
    hidden_own, total, part, core_in, plane_out, plane_in,
    w_sem, tok_send, tok_recv, cotan_send, cotan_recv, cotan_local, own_sem, sent_send, landed_recv,
    peer_send, peer_recv, grads_send, grads_recv, hidden_send, hidden_recv, out_sem,
    core_send, core_recv, plane_send, plane_recv,
):
    r, c, d = lax.axis_index("row"), lax.axis_index("col"), lax.axis_index("depth")
    other_d = 1 - d
    core = c + 1 - 2 * (c % 2)
    across = (c + 2) % 4
    pair = r + 1 - 2 * (r % 2)
    peer = 3 - r
    half = r // 2
    far = 1 - half
    chunks = weights.shape[0]
    width = chunks * LANES
    rows = tokens_ref.shape[0]
    block = 2 * rows
    group = 4 * rows

    def remote(src, dst, send, recv, **where):
        return pltpu.make_async_remote_copy(
            src_ref=src, dst_ref=dst, send_sem=send, recv_sem=recv,
            device_id={"row": r, "col": c, "depth": d, **where}, device_id_type=MESH,
        )

    def load(k, which):
        ref = (gate_ref, up_ref)[which]
        return pltpu.make_async_copy(
            ref.at[:, aligned(d * width + k * LANES, LANES)],
            weights.at[k, :, pl.ds(which * LANES, LANES)],
            w_sem.at[which, k],
        )

    @pl.loop(0, chunks)
    def _(k):
        load(k, 0).start()
        load(k, 1).start()

    barrier = pltpu.get_barrier_semaphore()
    partners = [dict(row=(r + step) % 4) for step in (1, 2, 3)] + [
        dict(row=pair, depth=other_d),
        dict(col=core),
        dict(col=across),
        dict(depth=other_d),
        dict(col=across, depth=other_d),
    ]
    for where in partners:
        pl.semaphore_signal(
            barrier, inc=1, device_id={"row": r, "col": c, "depth": d, **where},
            device_id_type=MESH,
        )
    pl.semaphore_wait(barrier, len(partners))

    def piece(row, depth):
        return tok.at[aligned(row * block + depth * rows, rows), :]

    is_root = c == r
    is_relay = across == r
    is_even = (c - r + 4) % 2 == 0

    def first_hop():
        return remote(
            tokens_ref, piece(r, d), tok_send.at[3, r * 2 + d], tok_recv.at[r * 2 + d], row=c
        )

    def forward(way, row, depth):
        where = (dict(col=across), dict(depth=other_d), dict(col=core))[way]
        at = row * 2 + depth
        return remote(
            piece(row, depth), piece(row, depth), tok_send.at[way, at], tok_recv.at[at], **where
        )

    def cotan_copy(depth, row):
        return remote(
            cotan_ref.at[:, aligned(depth * width, width)],
            cotan.at[aligned((r % 2) * block + d * rows, rows), :],
            cotan_send.at[depth], cotan_recv.at[(r % 2) * 2 + d], row=row, depth=depth,
        )

    def own_cotan():
        return pltpu.make_async_copy(
            cotan_ref.at[:, aligned(d * width, width)],
            cotan.at[aligned((r % 2) * block + d * rows, rows), :],
            cotan_local,
        )

    outer = (r == 0) | (r == 3)
    inner = (r == 1) | (r == 2)

    def own_tokens():
        return pltpu.make_async_copy(tokens_ref, piece(r, d), own_sem)

    @pl.when(c != r)
    def _():
        first_hop().start()

    @pl.when(outer)
    def _():
        cotan_copy(d, pair).start()
        cotan_copy(other_d, pair).start()

    @pl.when(inner)
    def _():
        own_cotan().start()
        cotan_copy(other_d, r).start()

    @pl.when(is_root)
    def _():
        own_tokens().start()
        own_tokens().wait()

    order = (r, pair, 3 - pair, peer)

    def near(step):
        row = order[step]

        def arrive():
            forward(0, row, d).wait_recv()

        if step == 0:
            pl.when(c != r)(arrive)
        else:
            arrive()

        @pl.when(is_root)
        def _():
            forward(0, row, d).start()

        @pl.when(is_even)
        def _():
            forward(1, row, d).start()
            forward(2, row, d).start()

    def away(step):
        row = order[step]
        forward(1, row, other_d).wait_recv()

        @pl.when(is_even)
        def _():
            forward(2, row, other_d).start()

    def partial(k, which):
        return jnp.dot(
            tok[aligned(which * group, group), :], weights[k], preferred_element_type=F32
        )

    def partials(k):
        both = jnp.dot(tok[...], weights[k], preferred_element_type=F32)
        return both.reshape(2, group, 2 * LANES)

    def weight_wait(k):
        load(k, 0).wait()
        load(k, 1).wait()

    def send_part(k, which):
        return remote(
            sent.at[k, which], landed.at[k, which], sent_send.at[k, which],
            landed_recv.at[k, which], row=pair,
        )

    near(0)
    near(1)

    away(0)
    away(1)

    @pl.when(outer)
    def _():
        weight_wait(0)
        sent[0, half] = partial(0, half).astype(BF16)
        send_part(0, half).start()

    near(2)
    away(2)
    near(3)
    away(3)

    def keep_tokens():
        return pltpu.make_async_copy(turned, every_tokens_ref, out_sem.at[0])

    def keep(k, which, kind):
        ref = (grad_gate_ref, grad_up_ref)[kind]
        return pltpu.make_async_copy(
            grads.at[k, which, :, pl.ds(kind * LANES, LANES)],
            ref.at[aligned(which * group, group), aligned(k * LANES, LANES)],
            out_sem.at[1 + kind],
        )

    def add_tokens_grad(k):
        for which in range(2):
            keep(k, which, 0).start()
            keep(k, which, 1).start()

        @pl.when(k % 2 == 1)
        def _():
            step = min(256, total.shape[1])
            for at in range(0, total.shape[1], step):
                term = jnp.zeros((2 * group, step), F32)
                for chunk in (k - 1, k):
                    term += lax.dot_general(
                        grads[chunk].reshape(2 * group, 2 * LANES),
                        weights[chunk, pl.ds(at, step), :],
                        (((1,), (1,)), ((), ())), preferred_element_type=F32,
                    )
                total[:, pl.ds(at, step)] += term

    total[...] = jnp.zeros_like(total)

    def send_peer(k):
        return remote(to_peer.at[k], from_peer.at[k], peer_send.at[k], peer_recv.at[k], row=peer)

    def send_grads(k, which, to, way):
        return remote(
            grads.at[k, which], grads.at[k, which], grads_send.at[way, k],
            grads_recv.at[k, which], row=to,
        )

    def send_hidden(way):
        row, depth = ((r, other_d), (pair, d), (pair, other_d))[way]
        return remote(
            hidden_rows.at[aligned((row % 2) * block + depth * rows, rows), :],
            hidden_own.at[:, aligned(d * width, width)],
            hidden_send.at[way], hidden_recv.at[d], row=row, depth=depth,
        )

    def hidden_arrived(depth):
        return remote(
            hidden_rows.at[pl.ds(0, rows), :], hidden_own.at[:, aligned(depth * width, width)],
            hidden_send.at[0], hidden_recv.at[depth],
        )

    def take_grads(k):
        send_grads(k, half, r, 0).wait_recv()
        send_grads(k, far, r, 0).wait_recv()
        add_tokens_grad(k)

    lag = min(8, chunks)
    flight = min(2, chunks)

    @pl.when(outer)
    def _():
        @pl.loop(0, chunks)
        def _(k):
            @pl.when(k >= 1)
            def _():
                weight_wait(k)

            @pl.when(k >= flight)
            def _():
                send_part(k - flight, far).wait_send()
                send_part(k - flight, half).wait_send()

            @pl.when(k == 0)
            def _():
                sent[k, far] = partial(k, far).astype(BF16)
                send_part(k, far).start()

            @pl.when(k >= 1)
            def _():
                sent[k] = partials(k).astype(BF16)
                send_part(k, far).start()
                send_part(k, half).start()

            @pl.when(k >= lag)
            def _():
                take_grads(k - lag)

        @pl.loop(chunks - lag, chunks)
        def _(k):
            take_grads(k)

        @pl.loop(chunks - flight, chunks)
        def _(k):
            send_part(k, far).wait_send()
            send_part(k, half).wait_send()

        cotan_copy(d, pair).wait_send()
        cotan_copy(other_d, pair).wait_send()

    @pl.when(inner)
    def _():
        def prepare(k):
            weight_wait(k)
            mine[...] = partials(k)

        def reduce_far(k):
            send_part(k, far).wait_recv()
            to_peer[k] = (mine[far] + landed[k, far].astype(F32)).astype(BF16)
            send_peer(k).start()

        def reduce_half(k):
            send_part(k, half).wait_recv()
            own_sum[k] = mine[half] + landed[k, half].astype(F32)

            @pl.when(k + 1 < chunks)
            def _():
                prepare(k + 1)

        def pointwise(k):
            @pl.when(k == 0)
            def _():
                own_cotan().wait()
                for row, depth in ((r, other_d), (pair, d), (pair, other_d)):
                    remote(
                        cotan_ref.at[:, pl.ds(0, width)],
                        cotan.at[aligned((row % 2) * block + depth * rows, rows), :],
                        cotan_send.at[0], cotan_recv.at[(row % 2) * 2 + depth],
                    ).wait_recv()

            send_peer(k).wait_recv()
            sums = own_sum[k] + from_peer[k].astype(F32)
            gate, up = sums[:, :LANES], sums[:, LANES:]
            cols = aligned(k * LANES, LANES)
            cot = cotan[:, cols].astype(F32)
            sigmoid = jax.nn.sigmoid(gate)
            silu = gate * sigmoid
            grads[k, half, :, pl.ds(0, LANES)] = (
                cot * up * sigmoid * (1.0 + gate * (1.0 - sigmoid))
            ).astype(BF16)
            grads[k, half, :, pl.ds(LANES, LANES)] = (cot * silu).astype(BF16)
            send_grads(k, half, peer, 0).start()
            send_grads(k, half, pair, 1).start()
            hidden_rows[:, cols] = (silu * up).astype(BF16)
            hidden_own[:, aligned(d * width + k * LANES, LANES)] = hidden_rows[
                aligned((r % 2) * block + d * rows, rows), cols
            ]

            @pl.when(k == chunks - 1)
            def _():
                send_hidden(0).start()

        def spread(k):
            send_grads(k, far, pair, 2).wait_recv()
            send_grads(k, far, pair, 2).start()

            @pl.when(k == chunks - 1)
            def _():
                send_hidden(1).start()
                send_hidden(2).start()

        prepare(0)

        @pl.loop(0, chunks + 2)
        def _(i):
            @pl.when(i < chunks)
            def _():
                reduce_far(i)

            @pl.when((i >= 1) & (i <= chunks))
            def _():
                pointwise(i - 1)

            @pl.when(i >= 2)
            def _():
                spread(i - 2)

            @pl.when(i < chunks)
            def _():
                reduce_half(i)

            @pl.when(i >= 2)
            def _():
                add_tokens_grad(i - 2)

        cotan_copy(other_d, r).wait_send()

    part[...] = total[...].astype(BF16)

    def core_copy(slot):
        col = (core, (core + 2) % 4)[slot]
        return remote(
            part.at[aligned(col * block, block), :], core_in.at[slot],
            core_send.at[slot], core_recv.at[slot], col=core,
        )

    core_copy(1).start()
    core_copy(0).start()
    turned[...] = tok[...].T
    keep_tokens().start()

    def plane_copy(way):
        where = (
            dict(col=across, depth=other_d), dict(col=across), dict(depth=other_d)
        )[way]
        depth = (other_d, d, other_d)[way]
        slot = (1, 1, 0)[way]
        return remote(
            plane_out.at[slot, aligned(depth * rows, rows), :], plane_in.at[way],
            plane_send.at[way], plane_recv.at[way], **where,
        )

    core_copy(1).wait_recv()
    plane_out[1] = (
        total[aligned(across * block, block), :] + core_in[1].astype(F32)
    ).astype(BF16)
    plane_copy(0).start()
    plane_copy(1).start()
    core_copy(0).wait_recv()
    plane_out[0] = (
        total[aligned(c * block, block), :] + core_in[0].astype(F32)
    ).astype(BF16)
    plane_copy(2).start()

    @pl.when(outer)
    def _():
        hidden_arrived(d).wait_recv()

    hidden_arrived(other_d).wait_recv()
    hidden_ref[...] = hidden_own[...]

    @pl.when(c != r)
    def _():
        first_hop().wait_send()

    for row in range(4):
        @pl.when(is_root)
        def _():
            forward(0, row, d).wait_send()

        @pl.when(is_even)
        def _():
            forward(1, row, d).wait_send()
            forward(2, row, d).wait_send()
            forward(2, row, other_d).wait_send()

    @pl.when(inner)
    def _():
        @pl.loop(0, chunks)
        def _(k):
            send_peer(k).wait_send()
            send_grads(k, half, peer, 0).wait_send()
            send_grads(k, half, pair, 1).wait_send()
            send_grads(k, far, pair, 2).wait_send()

        for way in range(3):
            send_hidden(way).wait_send()

    keep_tokens().wait()
    pltpu.make_async_copy(grad_gate_ref, grad_gate_ref, out_sem.at[1]).wait()
    pltpu.make_async_copy(grad_up_ref, grad_up_ref, out_sem.at[2]).wait()
    core_copy(0).wait_send()
    core_copy(1).wait_send()
    own = plane_out[0, aligned(d * rows, rows), :].astype(F32)
    for way in range(3):
        plane_copy(way).wait_recv()
        own = own + plane_in[way].astype(F32)
    grad_tokens_ref[...] = own.astype(BF16)
    for way in range(3):
        plane_copy(way).wait_send()


def exchange(tokens, gate_weight, up_weight, grad_hidden):
    rows, feats = tokens.shape
    cols = gate_weight.shape[1]
    chunks = cols // (2 * LANES)
    every = 8 * rows
    group = every // 2
    dma = pltpu.SemaphoreType.DMA
    vmem = pl.BlockSpec(memory_space=pltpu.VMEM)
    hbm = pl.BlockSpec(memory_space=pl.ANY)
    scratch = [
        pltpu.VMEM((every, feats), BF16),
        pltpu.VMEM((feats, every), BF16),
        pltpu.VMEM((chunks, feats, 2 * LANES), BF16),
        pltpu.VMEM((chunks, 2, group, 2 * LANES), BF16),
        pltpu.VMEM((chunks, 2, group, 2 * LANES), BF16),
        pltpu.VMEM((chunks, group, 2 * LANES), BF16),
        pltpu.VMEM((chunks, group, 2 * LANES), BF16),
        pltpu.VMEM((chunks, group, 2 * LANES), F32),
        pltpu.VMEM((2, group, 2 * LANES), F32),
        pltpu.VMEM((chunks, 2, group, 2 * LANES), BF16),
        pltpu.VMEM((group, cols // 2), BF16),
        pltpu.VMEM((group, cols // 2), BF16),
        pltpu.VMEM((rows, cols), BF16),
        pltpu.VMEM((every, feats), F32),
        pltpu.VMEM((every, feats), BF16),
        pltpu.VMEM((2, 2 * rows, feats), BF16),
        pltpu.VMEM((2, 2 * rows, feats), BF16),
        pltpu.VMEM((3, rows, feats), BF16),
        dma((2, chunks)),
        dma((4, 8)),
        dma((8,)),
        dma((2,)),
        dma((4,)),
        dma,
        dma,
        dma((chunks, 2)),
        dma((chunks, 2)),
        dma((chunks,)),
        dma((chunks,)),
        dma((3, chunks)),
        dma((chunks, 2)),
        dma((3,)),
        dma((2,)),
        dma((3,)),
        dma((2,)),
        dma((2,)),
        dma((3,)),
        dma((3,)),
    ]
    return pl.pallas_call(
        kernel,
        out_shape=(
            jax.ShapeDtypeStruct((rows, cols), BF16),
            jax.ShapeDtypeStruct((rows, feats), BF16),
            jax.ShapeDtypeStruct((feats, every), BF16),
            jax.ShapeDtypeStruct((every, cols // 2), BF16),
            jax.ShapeDtypeStruct((every, cols // 2), BF16),
        ),
        in_specs=[hbm, hbm, hbm, hbm],
        out_specs=(vmem, vmem, hbm, hbm, hbm),
        scratch_shapes=scratch,
        compiler_params=pltpu.CompilerParams(
            collective_id=0, has_side_effects=True, vmem_limit_bytes=60 * 2**20
        ),
        cost_estimate=pl.CostEstimate(
            flops=8 * every * feats * cols // 2, bytes_accessed=4 * feats * cols,
            transcendentals=group * cols // 2,
        ),
    )(tokens, gate_weight, up_weight, grad_hidden)


def weight_kernel(
    tokens_ref, gate_ref, up_ref, hidden_ref, grad_tokens_ref,
    hidden_out, grad_tokens_out, gate_out, up_out,
    tokens, gate, up, hidden, grad_tokens, made, sem, load_sem, grads_sem, carry_sem,
):
    width = 2 * LANES
    tiles = gate.shape[1] // width
    steps, step = made.shape[1:3]
    part = step // 2
    outs = (gate_out, up_out)
    carried = (
        (hidden_ref, hidden, hidden_out),
        (grad_tokens_ref, grad_tokens, grad_tokens_out),
    )

    def load_tokens(at):
        rows = pl.ds(at * step, step)
        return pltpu.make_async_copy(
            tokens_ref.at[rows, :], tokens.at[rows, :], load_sem.at[at]
        )

    def load_grads(which, at):
        cols = pl.ds(at * width, width)
        source, held = ((gate_ref, gate), (up_ref, up))[which]
        return pltpu.make_async_copy(
            source.at[:, cols], held.at[:, cols], grads_sem.at[which, at]
        )

    def carry(which, way):
        return pltpu.make_async_copy(
            carried[which][way], carried[which][way + 1], carry_sem.at[way, which]
        )

    def leave(at, which, piece):
        return pltpu.make_async_copy(
            made.at[which, at, pl.ds(piece * part, part), :],
            outs[which].at[pl.ds(at * step + piece * part, part), :],
            sem.at[which, at, piece],
        )

    load_tokens(0).start()
    for which in range(2):
        for tile in range(tiles):
            load_grads(which, tile).start()
    for at in range(1, steps):
        load_tokens(at).start()
    for which in range(2):
        carry(which, 0).start()
    for at in range(steps):
        load_tokens(at).wait()
        left = tokens[pl.ds(at * step, step), :]
        for which in range(2):
            for tile in range(tiles):
                if at == 0:
                    load_grads(which, tile).wait()
                cols = pl.ds(tile * width, width)
                made[which, at, :, cols] = jnp.dot(
                    left, (gate, up)[which][:, cols], preferred_element_type=F32
                )
            for piece in range(2):
                leave(at, which, piece).start()
        if at == 0:
            for which in range(2):
                carry(which, 0).wait()
                carry(which, 1).start()
    for at in range(steps):
        for which in range(2):
            for piece in range(2):
                leave(at, which, piece).wait()
    for which in range(2):
        carry(which, 1).wait()


def weight_grads(turned_tokens, grad_gate, grad_up, hidden, grad_tokens):
    feats, every = turned_tokens.shape
    cols = grad_gate.shape[1]
    steps = 4
    shape = jax.ShapeDtypeStruct((feats, cols), F32)
    hbm = pl.BlockSpec(memory_space=pl.ANY)
    return pl.pallas_call(
        weight_kernel,
        out_shape=(
            jax.ShapeDtypeStruct(hidden.shape, hidden.dtype),
            jax.ShapeDtypeStruct(grad_tokens.shape, grad_tokens.dtype),
            shape,
            shape,
        ),
        in_specs=[hbm, hbm, hbm, hbm, hbm],
        out_specs=(hbm, hbm, hbm, hbm),
        scratch_shapes=[
            pltpu.VMEM(turned_tokens.shape, BF16),
            pltpu.VMEM(grad_gate.shape, BF16),
            pltpu.VMEM(grad_up.shape, BF16),
            pltpu.VMEM(hidden.shape, BF16),
            pltpu.VMEM(grad_tokens.shape, BF16),
            pltpu.VMEM((2, steps, feats // steps, cols), F32),
            pltpu.SemaphoreType.DMA((2, steps, 2)),
            pltpu.SemaphoreType.DMA((steps,)),
            pltpu.SemaphoreType.DMA((2, cols // (2 * LANES))),
            pltpu.SemaphoreType.DMA((2, 2)),
        ],
        compiler_params=pltpu.CompilerParams(vmem_limit_bytes=60 * 2**20),
        cost_estimate=pl.CostEstimate(
            flops=4 * every * feats * cols, bytes_accessed=8 * feats * cols, transcendentals=0
        ),
    )(turned_tokens, grad_gate, grad_up, hidden, grad_tokens)


def on_line(tokens, gate_weight, up_weight, grad_hidden):
    hidden, grad_tokens, turned_tokens, grad_gate, grad_up = exchange(
        tokens, gate_weight, up_weight, grad_hidden
    )
    return weight_grads(turned_tokens, grad_gate, grad_up, hidden, grad_tokens)


def from_root(value, axis, source):
    kept = jnp.where(lax.axis_index(axis) == source, value, 0).astype(value.dtype)
    return lax.psum(kept, axis)


def local_grads(gate_pre, up_pre, cotangent):
    sigmoid_gate = jax.nn.sigmoid(gate_pre)
    cotan_f32 = cotangent.astype(jnp.float32)
    grad_gate = (
        cotan_f32 * up_pre * sigmoid_gate * (1.0 + gate_pre * (1.0 - sigmoid_gate))
    ).astype(jnp.bfloat16)
    grad_up = (cotan_f32 * jax.nn.silu(gate_pre)).astype(jnp.bfloat16)
    return (grad_gate, grad_up)


def matmul_f32(left, right):
    return jnp.dot(left, right, preferred_element_type=jnp.float32)


def rounded_term(left, right):
    return matmul_f32(left, right).astype(jnp.bfloat16).astype(jnp.float32)


def local(tokens, gate_weight, up_weight, grad_hidden):
    hidden_cols = gate_weight.shape[1]
    row_tokens = lax.all_gather(tokens, "row", axis=0, tiled=True)
    diag_panel = from_root(row_tokens, "col", lax.axis_index("row"))
    summed = lax.psum_scatter(
        jnp.concatenate(
            [rounded_term(diag_panel, gate_weight), rounded_term(diag_panel, up_weight)], 1
        ).astype(jnp.bfloat16),
        "row",
        scatter_dimension=0,
        tiled=True,
    ).astype(jnp.float32)
    gate_sum = summed[:, :hidden_cols]
    up_sum = summed[:, hidden_cols:]
    hidden = (jax.nn.silu(gate_sum) * up_sum).astype(jnp.bfloat16)
    own_gate, own_up = local_grads(gate_sum, up_sum, grad_hidden)
    grad_gate, grad_up = (
        lax.all_gather(own_gate, "row", axis=0, tiled=True),
        lax.all_gather(own_up, "row", axis=0, tiled=True),
    )
    first_term = jnp.einsum("tf,df->td", grad_gate, gate_weight, preferred_element_type=jnp.float32)
    grad_tokens = lax.psum_scatter(
        (
            first_term
            + jnp.einsum("tf,df->td", grad_up, up_weight, preferred_element_type=jnp.float32)
        ).astype(jnp.bfloat16),
        "col",
        scatter_dimension=0,
        tiled=True,
    )
    gate_slices, up_slices = (
        lax.all_to_all(grad_gate, "depth", split_axis=1, concat_axis=0, tiled=True),
        lax.all_to_all(grad_up, "depth", split_axis=1, concat_axis=0, tiled=True),
    )
    every_tokens = lax.all_gather(diag_panel, "depth", axis=0, tiled=True)
    grad_gate_weight = jnp.einsum(
        "td,tf->df", every_tokens, gate_slices, preferred_element_type=jnp.float32
    )
    grad_up_weight = jnp.einsum(
        "td,tf->df", every_tokens, up_slices, preferred_element_type=jnp.float32
    )
    return (hidden, grad_tokens, grad_gate_weight, grad_up_weight)


def pick(mesh, tokens, gate_weight, up_weight, grad_hidden):
    sizes = dict(mesh.shape)
    fits = (
        (sizes["row"], sizes["col"], sizes["depth"]) == (4, 4, 2)
        and tokens.shape[0] % 16 == 0
        and tokens.shape[1] % 128 == 0
        and gate_weight.shape[1] % (4 * LANES) == 0
    )
    plan = on_line if fits else local
    return plan(tokens, gate_weight, up_weight, grad_hidden)


def solution(mesh):
    return jax.shard_map(
        functools.partial(pick, mesh),
        mesh=mesh,
        in_specs=(
            P(("row", "depth"), "col"),
            P("row", "col"),
            P("row", "col"),
            P(("row", "depth"), "col"),
        ),
        out_specs=(
            P(("row", "depth"), "col"),
            P(("col", "depth"), "row"),
            P("row", ("col", "depth")),
            P("row", ("col", "depth")),
        ),
        check_vma=False,
    )
```

```python
import functools

import jax
import jax.numpy as jnp
from jax import lax
from jax.experimental import pallas as pl
from jax.experimental.pallas import tpu as pltpu
from jax.sharding import PartitionSpec as P

MESH = pl.DeviceIdType.MESH
LANES = 128
F32 = jnp.float32
BF16 = jnp.bfloat16


def aligned(start, size):
    return pl.ds(pl.multiple_of(start, size), size)


def kernel(
    tokens_ref, gate_ref, up_ref, cotan_ref,
    hidden_ref, grad_tokens_ref, every_tokens_ref, grad_gate_ref, grad_up_ref,
    tok, turned, weights, sent, landed, to_peer, from_peer, own_sum, mine, grads, cotan, hidden_rows,
    hidden_own, total, part, core_in, plane_out, plane_in,
    w_sem, tok_send, tok_recv, cotan_send, cotan_recv, cotan_local, own_sem, sent_send, landed_recv,
    peer_send, peer_recv, grads_send, grads_recv, hidden_send, hidden_recv, out_sem,
    core_send, core_recv, plane_send, plane_recv,
):
    r, c, d = lax.axis_index("row"), lax.axis_index("col"), lax.axis_index("depth")
    other_d = 1 - d
    core = c + 1 - 2 * (c % 2)
    across = (c + 2) % 4
    pair = r + 1 - 2 * (r % 2)
    peer = 3 - r
    half = r // 2
    far = 1 - half
    chunks = weights.shape[0]
    width = chunks * LANES
    rows = tokens_ref.shape[0]
    block = 2 * rows
    group = 4 * rows

    def remote(src, dst, send, recv, **where):
        return pltpu.make_async_remote_copy(
            src_ref=src, dst_ref=dst, send_sem=send, recv_sem=recv,
            device_id={"row": r, "col": c, "depth": d, **where}, device_id_type=MESH,
        )

    def load(k, which):
        ref = (gate_ref, up_ref)[which]
        return pltpu.make_async_copy(
            ref.at[:, aligned(d * width + k * LANES, LANES)],
            weights.at[k, :, pl.ds(which * LANES, LANES)],
            w_sem.at[which, k],
        )

    barrier = pltpu.get_barrier_semaphore()
    partners = [dict(row=(r + step) % 4) for step in (1, 2, 3)] + [
        dict(row=pair, depth=other_d),
        dict(col=core),
        dict(col=across),
        dict(depth=other_d),
        dict(col=across, depth=other_d),
    ]
    for where in partners:
        pl.semaphore_signal(
            barrier, inc=1, device_id={"row": r, "col": c, "depth": d, **where},
            device_id_type=MESH,
        )
    @pl.loop(0, chunks)
    def _(k):
        load(k, 0).start()
        load(k, 1).start()

    pl.semaphore_wait(barrier, len(partners))

    def piece(row, depth):
        return tok.at[aligned(row * block + depth * rows, rows), :]

    is_root = c == r
    is_relay = across == r
    is_even = (c - r + 4) % 2 == 0

    def first_hop():
        return remote(
            tokens_ref, piece(r, d), tok_send.at[3, r * 2 + d], tok_recv.at[r * 2 + d], row=c
        )

    def forward(way, row, depth):
        where = (dict(col=across), dict(depth=other_d), dict(col=core))[way]
        at = row * 2 + depth
        return remote(
            piece(row, depth), piece(row, depth), tok_send.at[way, at], tok_recv.at[at], **where
        )

    def cotan_copy(depth, row):
        return remote(
            cotan_ref.at[:, aligned(depth * width, width)],
            cotan.at[aligned((r % 2) * block + d * rows, rows), :],
            cotan_send.at[depth], cotan_recv.at[(r % 2) * 2 + d], row=row, depth=depth,
        )

    def own_cotan():
        return pltpu.make_async_copy(
            cotan_ref.at[:, aligned(d * width, width)],
            cotan.at[aligned((r % 2) * block + d * rows, rows), :],
            cotan_local,
        )

    outer = (r == 0) | (r == 3)
    inner = (r == 1) | (r == 2)

    def own_tokens():
        return pltpu.make_async_copy(tokens_ref, piece(r, d), own_sem)

    @pl.when(c != r)
    def _():
        first_hop().start()

    @pl.when(outer)
    def _():
        cotan_copy(d, pair).start()
        cotan_copy(other_d, pair).start()

    @pl.when(inner)
    def _():
        own_cotan().start()
        cotan_copy(other_d, r).start()

    @pl.when(is_root)
    def _():
        own_tokens().start()
        own_tokens().wait()

    order = (r, pair, 3 - pair, peer)

    def near(step):
        row = order[step]

        def arrive():
            forward(0, row, d).wait_recv()

        if step == 0:
            pl.when(c != r)(arrive)
        else:
            arrive()

        @pl.when(is_root)
        def _():
            forward(0, row, d).start()

        @pl.when(is_even)
        def _():
            forward(1, row, d).start()
            forward(2, row, d).start()

    def away(step):
        row = order[step]
        forward(1, row, other_d).wait_recv()

        @pl.when(is_even)
        def _():
            forward(2, row, other_d).start()

    def partial(k, which):
        return jnp.dot(
            tok[aligned(which * group, group), :], weights[k], preferred_element_type=F32
        )

    def partials(k):
        both = jnp.dot(tok[...], weights[k], preferred_element_type=F32)
        return both.reshape(2, group, 2 * LANES)

    def weight_wait(k):
        load(k, 0).wait()
        load(k, 1).wait()

    def send_part(k, which):
        return remote(
            sent.at[k, which], landed.at[k, which], sent_send.at[k, which],
            landed_recv.at[k, which], row=pair,
        )

    near(0)
    near(1)

    away(0)
    away(1)

    @pl.when(outer)
    def _():
        weight_wait(0)
        sent[0, half] = partial(0, half).astype(BF16)
        send_part(0, half).start()

    near(2)
    away(2)
    near(3)
    away(3)

    def keep_tokens():
        return pltpu.make_async_copy(turned, every_tokens_ref, out_sem.at[0])

    def keep(k, which, kind):
        ref = (grad_gate_ref, grad_up_ref)[kind]
        return pltpu.make_async_copy(
            grads.at[k, which, :, pl.ds(kind * LANES, LANES)],
            ref.at[aligned(which * group, group), aligned(k * LANES, LANES)],
            out_sem.at[1 + kind],
        )

    def add_tokens_grad(k):
        for which in range(2):
            keep(k, which, 0).start()
            keep(k, which, 1).start()

        @pl.when(k == chunks // 2)
        def _():
            turned[...] = tok[...].T
            keep_tokens().start()

        @pl.when(k % 2 == 1)
        def _():
            step = min(256, total.shape[1])
            for at in range(0, total.shape[1], step):
                term = jnp.zeros((2 * group, step), F32)
                for chunk in (k - 1, k):
                    term += lax.dot_general(
                        grads[chunk].reshape(2 * group, 2 * LANES),
                        weights[chunk, pl.ds(at, step), :],
                        (((1,), (1,)), ((), ())), preferred_element_type=F32,
                    )
                total[:, pl.ds(at, step)] += term

    total[...] = jnp.zeros_like(total)

    def send_peer(k):
        return remote(to_peer.at[k], from_peer.at[k], peer_send.at[k], peer_recv.at[k], row=peer)

    def send_grads(k, which, to, way):
        return remote(
            grads.at[k, which], grads.at[k, which], grads_send.at[way, k],
            grads_recv.at[k, which], row=to,
        )

    def send_hidden(way):
        row, depth = ((r, other_d), (pair, d), (pair, other_d))[way]
        return remote(
            hidden_rows.at[aligned((row % 2) * block + depth * rows, rows), :],
            hidden_own.at[:, aligned(d * width, width)],
            hidden_send.at[way], hidden_recv.at[d], row=row, depth=depth,
        )

    def hidden_arrived(depth):
        return remote(
            hidden_rows.at[pl.ds(0, rows), :], hidden_own.at[:, aligned(depth * width, width)],
            hidden_send.at[0], hidden_recv.at[depth],
        )

    def take_grads(k):
        send_grads(k, half, r, 0).wait_recv()
        send_grads(k, far, r, 0).wait_recv()
        add_tokens_grad(k)

    lag = min(8, chunks)
    flight = min(2, chunks)

    @pl.when(outer)
    def _():
        @pl.loop(0, chunks)
        def _(k):
            @pl.when(k >= 1)
            def _():
                weight_wait(k)

            @pl.when(k >= flight)
            def _():
                send_part(k - flight, far).wait_send()
                send_part(k - flight, half).wait_send()

            @pl.when(k == 0)
            def _():
                sent[k, far] = partial(k, far).astype(BF16)
                send_part(k, far).start()

            @pl.when(k >= 1)
            def _():
                sent[k] = partials(k).astype(BF16)
                send_part(k, far).start()
                send_part(k, half).start()

            @pl.when(k >= lag)
            def _():
                take_grads(k - lag)

        @pl.loop(chunks - lag, chunks)
        def _(k):
            take_grads(k)

        @pl.loop(chunks - flight, chunks)
        def _(k):
            send_part(k, far).wait_send()
            send_part(k, half).wait_send()

        cotan_copy(d, pair).wait_send()
        cotan_copy(other_d, pair).wait_send()

    @pl.when(inner)
    def _():
        def prepare(k):
            weight_wait(k)
            mine[...] = partials(k)

        def reduce_far(k):
            send_part(k, far).wait_recv()
            to_peer[k] = (mine[far] + landed[k, far].astype(F32)).astype(BF16)
            send_peer(k).start()

        def reduce_half(k):
            send_part(k, half).wait_recv()
            own_sum[k] = mine[half] + landed[k, half].astype(F32)

            @pl.when(k + 1 < chunks)
            def _():
                prepare(k + 1)

        def pointwise(k):
            @pl.when(k == 0)
            def _():
                own_cotan().wait()
                for row, depth in ((r, other_d), (pair, d), (pair, other_d)):
                    remote(
                        cotan_ref.at[:, pl.ds(0, width)],
                        cotan.at[aligned((row % 2) * block + depth * rows, rows), :],
                        cotan_send.at[0], cotan_recv.at[(row % 2) * 2 + depth],
                    ).wait_recv()

            send_peer(k).wait_recv()
            sums = own_sum[k] + from_peer[k].astype(F32)
            gate, up = sums[:, :LANES], sums[:, LANES:]
            cols = aligned(k * LANES, LANES)
            cot = cotan[:, cols].astype(F32)
            sigmoid = jax.nn.sigmoid(gate)
            silu = gate * sigmoid
            grads[k, half, :, pl.ds(0, LANES)] = (
                cot * up * sigmoid * (1.0 + gate * (1.0 - sigmoid))
            ).astype(BF16)
            grads[k, half, :, pl.ds(LANES, LANES)] = (cot * silu).astype(BF16)
            send_grads(k, half, peer, 0).start()
            send_grads(k, half, pair, 1).start()
            hidden_rows[:, cols] = (silu * up).astype(BF16)
            hidden_own[:, aligned(d * width + k * LANES, LANES)] = hidden_rows[
                aligned((r % 2) * block + d * rows, rows), cols
            ]

            @pl.when(k == chunks - 1)
            def _():
                send_hidden(0).start()

        def spread(k):
            send_grads(k, far, pair, 2).wait_recv()
            send_grads(k, far, pair, 2).start()

        prepare(0)

        @pl.loop(0, chunks + 2)
        def _(i):
            @pl.when(i < chunks)
            def _():
                reduce_far(i)

            @pl.when((i >= 1) & (i <= chunks))
            def _():
                pointwise(i - 1)

            @pl.when(i >= 2)
            def _():
                spread(i - 2)

            @pl.when(i < chunks)
            def _():
                reduce_half(i)

            @pl.when(i >= 2)
            def _():
                add_tokens_grad(i - 2)

        send_grads(chunks - 1, far, pair, 2).wait_send()
        send_hidden(1).start()
        send_hidden(2).start()
        cotan_copy(other_d, r).wait_send()

    part[...] = total[...].astype(BF16)

    def core_copy(slot):
        col = (core, (core + 2) % 4)[slot]
        return remote(
            part.at[aligned(col * block, block), :], core_in.at[slot],
            core_send.at[slot], core_recv.at[slot], col=core,
        )

    core_copy(1).start()
    core_copy(0).start()

    def plane_copy(way):
        where = (
            dict(col=across, depth=other_d), dict(col=across), dict(depth=other_d)
        )[way]
        depth = (other_d, d, other_d)[way]
        slot = (1, 1, 0)[way]
        return remote(
            plane_out.at[slot, aligned(depth * rows, rows), :], plane_in.at[way],
            plane_send.at[way], plane_recv.at[way], **where,
        )

    core_copy(1).wait_recv()
    plane_out[1] = (
        total[aligned(across * block, block), :] + core_in[1].astype(F32)
    ).astype(BF16)
    plane_copy(0).start()
    plane_copy(1).start()
    core_copy(0).wait_recv()
    plane_out[0] = (
        total[aligned(c * block, block), :] + core_in[0].astype(F32)
    ).astype(BF16)
    plane_copy(2).start()

    @pl.when(outer)
    def _():
        hidden_arrived(d).wait_recv()

    hidden_arrived(other_d).wait_recv()
    hidden_ref[...] = hidden_own[...]

    @pl.when(c != r)
    def _():
        first_hop().wait_send()

    for row in range(4):
        @pl.when(is_root)
        def _():
            forward(0, row, d).wait_send()

        @pl.when(is_even)
        def _():
            forward(1, row, d).wait_send()
            forward(2, row, d).wait_send()
            forward(2, row, other_d).wait_send()

    @pl.when(inner)
    def _():
        @pl.loop(0, chunks)
        def _(k):
            send_peer(k).wait_send()
            send_grads(k, half, peer, 0).wait_send()
            send_grads(k, half, pair, 1).wait_send()

            @pl.when(k < chunks - 1)
            def _():
                send_grads(k, far, pair, 2).wait_send()

        for way in range(3):
            send_hidden(way).wait_send()

    keep_tokens().wait()
    pltpu.make_async_copy(grad_gate_ref, grad_gate_ref, out_sem.at[1]).wait()
    pltpu.make_async_copy(grad_up_ref, grad_up_ref, out_sem.at[2]).wait()
    core_copy(0).wait_send()
    core_copy(1).wait_send()
    own = plane_out[0, aligned(d * rows, rows), :].astype(F32)
    for way in range(3):
        plane_copy(way).wait_recv()
        own = own + plane_in[way].astype(F32)
    grad_tokens_ref[...] = own.astype(BF16)
    for way in range(3):
        plane_copy(way).wait_send()


def exchange(tokens, gate_weight, up_weight, grad_hidden):
    rows, feats = tokens.shape
    cols = gate_weight.shape[1]
    chunks = cols // (2 * LANES)
    every = 8 * rows
    group = every // 2
    dma = pltpu.SemaphoreType.DMA
    vmem = pl.BlockSpec(memory_space=pltpu.VMEM)
    hbm = pl.BlockSpec(memory_space=pl.ANY)
    scratch = [
        pltpu.VMEM((every, feats), BF16),
        pltpu.VMEM((feats, every), BF16),
        pltpu.VMEM((chunks, feats, 2 * LANES), BF16),
        pltpu.VMEM((chunks, 2, group, 2 * LANES), BF16),
        pltpu.VMEM((chunks, 2, group, 2 * LANES), BF16),
        pltpu.VMEM((chunks, group, 2 * LANES), BF16),
        pltpu.VMEM((chunks, group, 2 * LANES), BF16),
        pltpu.VMEM((chunks, group, 2 * LANES), F32),
        pltpu.VMEM((2, group, 2 * LANES), F32),
        pltpu.VMEM((chunks, 2, group, 2 * LANES), BF16),
        pltpu.VMEM((group, cols // 2), BF16),
        pltpu.VMEM((group, cols // 2), BF16),
        pltpu.VMEM((rows, cols), BF16),
        pltpu.VMEM((every, feats), F32),
        pltpu.VMEM((every, feats), BF16),
        pltpu.VMEM((2, 2 * rows, feats), BF16),
        pltpu.VMEM((2, 2 * rows, feats), BF16),
        pltpu.VMEM((3, rows, feats), BF16),
        dma((2, chunks)),
        dma((4, 8)),
        dma((8,)),
        dma((2,)),
        dma((4,)),
        dma,
        dma,
        dma((chunks, 2)),
        dma((chunks, 2)),
        dma((chunks,)),
        dma((chunks,)),
        dma((3, chunks)),
        dma((chunks, 2)),
        dma((3,)),
        dma((2,)),
        dma((3,)),
        dma((2,)),
        dma((2,)),
        dma((3,)),
        dma((3,)),
    ]
    return pl.pallas_call(
        kernel,
        out_shape=(
            jax.ShapeDtypeStruct((rows, cols), BF16),
            jax.ShapeDtypeStruct((rows, feats), BF16),
            jax.ShapeDtypeStruct((feats, every), BF16),
            jax.ShapeDtypeStruct((every, cols // 2), BF16),
            jax.ShapeDtypeStruct((every, cols // 2), BF16),
        ),
        in_specs=[hbm, hbm, hbm, hbm],
        out_specs=(vmem, vmem, hbm, hbm, hbm),
        scratch_shapes=scratch,
        compiler_params=pltpu.CompilerParams(
            collective_id=0, has_side_effects=True, vmem_limit_bytes=60 * 2**20
        ),
        cost_estimate=pl.CostEstimate(
            flops=8 * every * feats * cols // 2, bytes_accessed=4 * feats * cols,
            transcendentals=group * cols // 2,
        ),
    )(tokens, gate_weight, up_weight, grad_hidden)


def weight_kernel(
    tokens_ref, gate_ref, up_ref, hidden_ref, grad_tokens_ref,
    hidden_out, grad_tokens_out, gate_out, up_out,
    tokens, gate, up, hidden, grad_tokens, made, sem, load_sem, grads_sem, carry_sem,
):
    width = 2 * LANES
    tiles = gate.shape[1] // width
    steps, step = made.shape[1:3]
    part = step // 2
    outs = (gate_out, up_out)
    carried = (
        (hidden_ref, hidden, hidden_out),
        (grad_tokens_ref, grad_tokens, grad_tokens_out),
    )

    def load_tokens(at):
        rows = pl.ds(at * step, step)
        return pltpu.make_async_copy(
            tokens_ref.at[rows, :], tokens.at[rows, :], load_sem.at[at]
        )

    def load_grads(which, at):
        cols = pl.ds(at * width, width)
        source, held = ((gate_ref, gate), (up_ref, up))[which]
        return pltpu.make_async_copy(
            source.at[:, cols], held.at[:, cols], grads_sem.at[which, at]
        )

    def carry(which, way):
        return pltpu.make_async_copy(
            carried[which][way], carried[which][way + 1], carry_sem.at[way, which]
        )

    def leave(at, which, piece):
        return pltpu.make_async_copy(
            made.at[which, at, pl.ds(piece * part, part), :],
            outs[which].at[pl.ds(at * step + piece * part, part), :],
            sem.at[which, at, piece],
        )

    load_tokens(0).start()
    for which in range(2):
        for tile in range(tiles):
            load_grads(which, tile).start()
    for at in range(1, steps):
        load_tokens(at).start()
    for which in range(2):
        carry(which, 0).start()
    for at in range(steps):
        load_tokens(at).wait()
        left = tokens[pl.ds(at * step, step), :]
        for which in range(2):
            for tile in range(tiles):
                if at == 0:
                    load_grads(which, tile).wait()
                cols = pl.ds(tile * width, width)
                made[which, at, :, cols] = jnp.dot(
                    left, (gate, up)[which][:, cols], preferred_element_type=F32
                )
            for piece in range(2):
                leave(at, which, piece).start()
        if at == 0:
            for which in range(2):
                carry(which, 0).wait()
                carry(which, 1).start()
    for at in range(steps):
        for which in range(2):
            for piece in range(2):
                leave(at, which, piece).wait()
    for which in range(2):
        carry(which, 1).wait()


def weight_grads(turned_tokens, grad_gate, grad_up, hidden, grad_tokens):
    feats, every = turned_tokens.shape
    cols = grad_gate.shape[1]
    steps = 4
    shape = jax.ShapeDtypeStruct((feats, cols), F32)
    hbm = pl.BlockSpec(memory_space=pl.ANY)
    return pl.pallas_call(
        weight_kernel,
        out_shape=(
            jax.ShapeDtypeStruct(hidden.shape, hidden.dtype),
            jax.ShapeDtypeStruct(grad_tokens.shape, grad_tokens.dtype),
            shape,
            shape,
        ),
        in_specs=[hbm, hbm, hbm, hbm, hbm],
        out_specs=(hbm, hbm, hbm, hbm),
        scratch_shapes=[
            pltpu.VMEM(turned_tokens.shape, BF16),
            pltpu.VMEM(grad_gate.shape, BF16),
            pltpu.VMEM(grad_up.shape, BF16),
            pltpu.VMEM(hidden.shape, BF16),
            pltpu.VMEM(grad_tokens.shape, BF16),
            pltpu.VMEM((2, steps, feats // steps, cols), F32),
            pltpu.SemaphoreType.DMA((2, steps, 2)),
            pltpu.SemaphoreType.DMA((steps,)),
            pltpu.SemaphoreType.DMA((2, cols // (2 * LANES))),
            pltpu.SemaphoreType.DMA((2, 2)),
        ],
        compiler_params=pltpu.CompilerParams(vmem_limit_bytes=60 * 2**20),
        cost_estimate=pl.CostEstimate(
            flops=4 * every * feats * cols, bytes_accessed=8 * feats * cols, transcendentals=0
        ),
    )(turned_tokens, grad_gate, grad_up, hidden, grad_tokens)


def on_line(tokens, gate_weight, up_weight, grad_hidden):
    hidden, grad_tokens, turned_tokens, grad_gate, grad_up = exchange(
        tokens, gate_weight, up_weight, grad_hidden
    )
    return weight_grads(turned_tokens, grad_gate, grad_up, hidden, grad_tokens)


def from_root(value, axis, source):
    kept = jnp.where(lax.axis_index(axis) == source, value, 0).astype(value.dtype)
    return lax.psum(kept, axis)


def local_grads(gate_pre, up_pre, cotangent):
    sigmoid_gate = jax.nn.sigmoid(gate_pre)
    cotan_f32 = cotangent.astype(jnp.float32)
    grad_gate = (
        cotan_f32 * up_pre * sigmoid_gate * (1.0 + gate_pre * (1.0 - sigmoid_gate))
    ).astype(jnp.bfloat16)
    grad_up = (cotan_f32 * jax.nn.silu(gate_pre)).astype(jnp.bfloat16)
    return (grad_gate, grad_up)


def matmul_f32(left, right):
    return jnp.dot(left, right, preferred_element_type=jnp.float32)


def rounded_term(left, right):
    return matmul_f32(left, right).astype(jnp.bfloat16).astype(jnp.float32)


def local(tokens, gate_weight, up_weight, grad_hidden):
    hidden_cols = gate_weight.shape[1]
    row_tokens = lax.all_gather(tokens, "row", axis=0, tiled=True)
    diag_panel = from_root(row_tokens, "col", lax.axis_index("row"))
    summed = lax.psum_scatter(
        jnp.concatenate(
            [rounded_term(diag_panel, gate_weight), rounded_term(diag_panel, up_weight)], 1
        ).astype(jnp.bfloat16),
        "row",
        scatter_dimension=0,
        tiled=True,
    ).astype(jnp.float32)
    gate_sum = summed[:, :hidden_cols]
    up_sum = summed[:, hidden_cols:]
    hidden = (jax.nn.silu(gate_sum) * up_sum).astype(jnp.bfloat16)
    own_gate, own_up = local_grads(gate_sum, up_sum, grad_hidden)
    grad_gate, grad_up = (
        lax.all_gather(own_gate, "row", axis=0, tiled=True),
        lax.all_gather(own_up, "row", axis=0, tiled=True),
    )
    first_term = jnp.einsum("tf,df->td", grad_gate, gate_weight, preferred_element_type=jnp.float32)
    grad_tokens = lax.psum_scatter(
        (
            first_term
            + jnp.einsum("tf,df->td", grad_up, up_weight, preferred_element_type=jnp.float32)
        ).astype(jnp.bfloat16),
        "col",
        scatter_dimension=0,
        tiled=True,
    )
    gate_slices, up_slices = (
        lax.all_to_all(grad_gate, "depth", split_axis=1, concat_axis=0, tiled=True),
        lax.all_to_all(grad_up, "depth", split_axis=1, concat_axis=0, tiled=True),
    )
    every_tokens = lax.all_gather(diag_panel, "depth", axis=0, tiled=True)
    grad_gate_weight = jnp.einsum(
        "td,tf->df", every_tokens, gate_slices, preferred_element_type=jnp.float32
    )
    grad_up_weight = jnp.einsum(
        "td,tf->df", every_tokens, up_slices, preferred_element_type=jnp.float32
    )
    return (hidden, grad_tokens, grad_gate_weight, grad_up_weight)


def pick(mesh, tokens, gate_weight, up_weight, grad_hidden):
    sizes = dict(mesh.shape)
    fits = (
        (sizes["row"], sizes["col"], sizes["depth"]) == (4, 4, 2)
        and tokens.shape[0] % 16 == 0
        and tokens.shape[1] % 128 == 0
        and gate_weight.shape[1] % (4 * LANES) == 0
    )
    plan = on_line if fits else local
    return plan(tokens, gate_weight, up_weight, grad_hidden)


def solution(mesh):
    return jax.shard_map(
        functools.partial(pick, mesh),
        mesh=mesh,
        in_specs=(
            P(("row", "depth"), "col"),
            P("row", "col"),
            P("row", "col"),
            P(("row", "depth"), "col"),
        ),
        out_specs=(
            P(("row", "depth"), "col"),
            P(("col", "depth"), "row"),
            P("row", ("col", "depth")),
            P("row", ("col", "depth")),
        ),
        check_vma=False,
    )
```

```python
import functools

import jax
import jax.numpy as jnp
from jax import lax
from jax.experimental import pallas as pl
from jax.experimental.pallas import tpu as pltpu
from jax.sharding import PartitionSpec as P

MESH = pl.DeviceIdType.MESH
LANES = 128
F32 = jnp.float32
BF16 = jnp.bfloat16


def aligned(start, size):
    return pl.ds(pl.multiple_of(start, size), size)


def kernel(
    tokens_ref, gate_ref, up_ref, cotan_ref,
    hidden_ref, grad_tokens_ref, every_tokens_ref, grad_gate_ref, grad_up_ref,
    tok, turned, weights, sent, landed, to_peer, from_peer, own_sum, mine, grads, cotan, hidden_rows,
    hidden_own, total, part, core_in, plane_out, plane_in,
    w_sem, tok_send, tok_recv, cotan_send, cotan_recv, cotan_local, own_sem, sent_send, landed_recv,
    peer_send, peer_recv, grads_send, grads_recv, hidden_send, hidden_recv, out_sem,
    core_send, core_recv, plane_send, plane_recv,
):
    r, c, d = lax.axis_index("row"), lax.axis_index("col"), lax.axis_index("depth")
    other_d = 1 - d
    core = c + 1 - 2 * (c % 2)
    across = (c + 2) % 4
    pair = r + 1 - 2 * (r % 2)
    peer = 3 - r
    half = r // 2
    far = 1 - half
    chunks = weights.shape[0]
    width = chunks * LANES
    rows = tokens_ref.shape[0]
    block = 2 * rows
    group = 4 * rows

    def remote(src, dst, send, recv, **where):
        return pltpu.make_async_remote_copy(
            src_ref=src, dst_ref=dst, send_sem=send, recv_sem=recv,
            device_id={"row": r, "col": c, "depth": d, **where}, device_id_type=MESH,
        )

    def load(k, which):
        ref = (gate_ref, up_ref)[which]
        return pltpu.make_async_copy(
            ref.at[:, aligned(d * width + k * LANES, LANES)],
            weights.at[k, :, pl.ds(which * LANES, LANES)],
            w_sem.at[which, k],
        )

    barrier = pltpu.get_barrier_semaphore()
    partners = [dict(row=(r + step) % 4) for step in (1, 2, 3)] + [
        dict(row=pair, depth=other_d),
        dict(col=core),
        dict(col=across),
        dict(depth=other_d),
        dict(col=across, depth=other_d),
    ]
    for where in partners:
        pl.semaphore_signal(
            barrier, inc=1, device_id={"row": r, "col": c, "depth": d, **where},
            device_id_type=MESH,
        )
    @pl.loop(0, chunks)
    def _(k):
        load(k, 0).start()
        load(k, 1).start()

    pl.semaphore_wait(barrier, len(partners))

    def piece(row, depth):
        return tok.at[aligned(row * block + depth * rows, rows), :]

    is_root = c == r
    is_relay = across == r
    is_even = (c - r + 4) % 2 == 0

    def first_hop():
        return remote(
            tokens_ref, piece(r, d), tok_send.at[3, r * 2 + d], tok_recv.at[r * 2 + d], row=c
        )

    def forward(way, row, depth):
        where = (dict(col=across), dict(depth=other_d), dict(col=core))[way]
        at = row * 2 + depth
        return remote(
            piece(row, depth), piece(row, depth), tok_send.at[way, at], tok_recv.at[at], **where
        )

    def cotan_copy(depth, row):
        return remote(
            cotan_ref.at[:, aligned(depth * width, width)],
            cotan.at[aligned((r % 2) * block + d * rows, rows), :],
            cotan_send.at[depth], cotan_recv.at[(r % 2) * 2 + d], row=row, depth=depth,
        )

    def own_cotan():
        return pltpu.make_async_copy(
            cotan_ref.at[:, aligned(d * width, width)],
            cotan.at[aligned((r % 2) * block + d * rows, rows), :],
            cotan_local,
        )

    outer = (r == 0) | (r == 3)
    inner = (r == 1) | (r == 2)

    def own_tokens():
        return pltpu.make_async_copy(tokens_ref, piece(r, d), own_sem)

    @pl.when(c != r)
    def _():
        first_hop().start()

    @pl.when(outer)
    def _():
        cotan_copy(d, pair).start()
        cotan_copy(other_d, pair).start()

    @pl.when(inner)
    def _():
        own_cotan().start()
        cotan_copy(other_d, r).start()

    @pl.when(is_root)
    def _():
        own_tokens().start()
        own_tokens().wait()

    order = (r, pair, 3 - pair, peer)

    def near(step):
        row = order[step]

        def arrive():
            forward(0, row, d).wait_recv()

        if step == 0:
            pl.when(c != r)(arrive)
        else:
            arrive()

        @pl.when(is_root)
        def _():
            forward(0, row, d).start()

        @pl.when(is_even)
        def _():
            forward(1, row, d).start()
            forward(2, row, d).start()

    def away(step):
        row = order[step]
        forward(1, row, other_d).wait_recv()

        @pl.when(is_even)
        def _():
            forward(2, row, other_d).start()

    def partial(k, which):
        return jnp.dot(
            tok[aligned(which * group, group), :], weights[k], preferred_element_type=F32
        )

    def partials(k):
        both = jnp.dot(tok[...], weights[k], preferred_element_type=F32)
        return both.reshape(2, group, 2 * LANES)

    def weight_wait(k):
        load(k, 0).wait()
        load(k, 1).wait()

    def send_part(k, which):
        return remote(
            sent.at[k, which], landed.at[k, which], sent_send.at[k, which],
            landed_recv.at[k, which], row=pair,
        )

    near(0)
    near(1)

    away(0)
    away(1)

    @pl.when(outer)
    def _():
        weight_wait(0)
        sent[0, half] = partial(0, half).astype(BF16)
        send_part(0, half).start()

    near(2)
    away(2)
    near(3)
    away(3)

    def keep_tokens():
        return pltpu.make_async_copy(turned, every_tokens_ref, out_sem.at[0])

    def keep(k, which, kind):
        ref = (grad_gate_ref, grad_up_ref)[kind]
        return pltpu.make_async_copy(
            grads.at[k, which, :, pl.ds(kind * LANES, LANES)],
            ref.at[aligned(which * group, group), aligned(k * LANES, LANES)],
            out_sem.at[1 + kind],
        )

    def add_tokens_grad(k):
        for which in range(2):
            keep(k, which, 0).start()
            keep(k, which, 1).start()

        @pl.when(k == chunks // 2)
        def _():
            turned[...] = tok[...].T
            keep_tokens().start()

        @pl.when(k % 2 == 1)
        def _():
            step = min(256, total.shape[1])
            for at in range(0, total.shape[1], step):
                term = jnp.zeros((2 * group, step), F32)
                for chunk in (k - 1, k):
                    term += lax.dot_general(
                        grads[chunk].reshape(2 * group, 2 * LANES),
                        weights[chunk, pl.ds(at, step), :],
                        (((1,), (1,)), ((), ())), preferred_element_type=F32,
                    )
                total[:, pl.ds(at, step)] += term

    total[...] = jnp.zeros_like(total)

    def send_peer(k):
        return remote(to_peer.at[k], from_peer.at[k], peer_send.at[k], peer_recv.at[k], row=peer)

    def send_grads(k, which, to, way):
        return remote(
            grads.at[k, which], grads.at[k, which], grads_send.at[way, k],
            grads_recv.at[k, which], row=to,
        )

    def send_hidden(way):
        row, depth = ((r, other_d), (pair, d), (pair, other_d))[way]
        return remote(
            hidden_rows.at[aligned((row % 2) * block + depth * rows, rows), :],
            hidden_own.at[:, aligned(d * width, width)],
            hidden_send.at[way], hidden_recv.at[d], row=row, depth=depth,
        )

    def hidden_arrived(depth):
        return remote(
            hidden_rows.at[pl.ds(0, rows), :], hidden_own.at[:, aligned(depth * width, width)],
            hidden_send.at[0], hidden_recv.at[depth],
        )

    def take_grads(k):
        send_grads(k, half, r, 0).wait_recv()
        send_grads(k, far, r, 0).wait_recv()
        add_tokens_grad(k)

    lag = min(8, chunks)
    flight = min(2, chunks)

    @pl.when(outer)
    def _():
        @pl.loop(0, chunks)
        def _(k):
            @pl.when(k >= 1)
            def _():
                weight_wait(k)

            @pl.when(k >= flight)
            def _():
                send_part(k - flight, far).wait_send()
                send_part(k - flight, half).wait_send()

            @pl.when(k == 0)
            def _():
                sent[k, far] = partial(k, far).astype(BF16)
                send_part(k, far).start()

            @pl.when(k >= 1)
            def _():
                sent[k] = partials(k).astype(BF16)
                send_part(k, far).start()
                send_part(k, half).start()

            @pl.when(k >= lag)
            def _():
                take_grads(k - lag)

        @pl.loop(chunks - lag, chunks)
        def _(k):
            take_grads(k)

        @pl.loop(chunks - flight, chunks)
        def _(k):
            send_part(k, far).wait_send()
            send_part(k, half).wait_send()

        cotan_copy(d, pair).wait_send()
        cotan_copy(other_d, pair).wait_send()

    @pl.when(inner)
    def _():
        def prepare(k):
            weight_wait(k)
            mine[...] = partials(k)

        def reduce_far(k):
            send_part(k, far).wait_recv()
            to_peer[k] = (mine[far] + landed[k, far].astype(F32)).astype(BF16)
            send_peer(k).start()

        def reduce_half(k):
            send_part(k, half).wait_recv()
            own_sum[k] = mine[half] + landed[k, half].astype(F32)

            @pl.when(k + 1 < chunks)
            def _():
                prepare(k + 1)

        def pointwise(k):
            @pl.when(k == 0)
            def _():
                own_cotan().wait()
                for row, depth in ((r, other_d), (pair, d), (pair, other_d)):
                    remote(
                        cotan_ref.at[:, pl.ds(0, width)],
                        cotan.at[aligned((row % 2) * block + depth * rows, rows), :],
                        cotan_send.at[0], cotan_recv.at[(row % 2) * 2 + depth],
                    ).wait_recv()

            send_peer(k).wait_recv()
            sums = own_sum[k] + from_peer[k].astype(F32)
            gate, up = sums[:, :LANES], sums[:, LANES:]
            cols = aligned(k * LANES, LANES)
            cot = cotan[:, cols].astype(F32)
            sigmoid = jax.nn.sigmoid(gate)
            silu = gate * sigmoid
            grads[k, half, :, pl.ds(0, LANES)] = (
                cot * up * sigmoid * (1.0 + gate * (1.0 - sigmoid))
            ).astype(BF16)
            grads[k, half, :, pl.ds(LANES, LANES)] = (cot * silu).astype(BF16)
            send_grads(k, half, peer, 0).start()
            send_grads(k, half, pair, 1).start()
            hidden_rows[:, cols] = (silu * up).astype(BF16)
            hidden_own[:, aligned(d * width + k * LANES, LANES)] = hidden_rows[
                aligned((r % 2) * block + d * rows, rows), cols
            ]

            @pl.when(k == chunks - 1)
            def _():
                send_hidden(0).start()

        def spread(k):
            send_grads(k, far, pair, 2).wait_recv()
            send_grads(k, far, pair, 2).start()

        prepare(0)

        @pl.loop(0, chunks + 2)
        def _(i):
            @pl.when(i < chunks)
            def _():
                reduce_far(i)

            @pl.when((i >= 1) & (i <= chunks))
            def _():
                pointwise(i - 1)

            @pl.when(i >= 2)
            def _():
                spread(i - 2)

            @pl.when(i < chunks)
            def _():
                reduce_half(i)

            @pl.when(i >= 2)
            def _():
                add_tokens_grad(i - 2)

        send_grads(chunks - 1, far, pair, 2).wait_send()
        send_hidden(1).start()
        send_hidden(2).start()
        cotan_copy(other_d, r).wait_send()

    part[...] = total[...].astype(BF16)

    def core_copy(slot):
        col = (core, (core + 2) % 4)[slot]
        return remote(
            part.at[aligned(col * block, block), :], core_in.at[slot],
            core_send.at[slot], core_recv.at[slot], col=core,
        )

    core_copy(1).start()
    core_copy(0).start()

    def plane_copy(way):
        where = (
            dict(col=across, depth=other_d), dict(col=across), dict(depth=other_d)
        )[way]
        depth = (other_d, d, other_d)[way]
        slot = (1, 1, 0)[way]
        return remote(
            plane_out.at[slot, aligned(depth * rows, rows), :], plane_in.at[way],
            plane_send.at[way], plane_recv.at[way], **where,
        )

    core_copy(1).wait_recv()
    plane_out[1] = (
        total[aligned(across * block, block), :] + core_in[1].astype(F32)
    ).astype(BF16)
    plane_copy(0).start()
    plane_copy(1).start()
    core_copy(0).wait_recv()
    plane_out[0] = (
        total[aligned(c * block, block), :] + core_in[0].astype(F32)
    ).astype(BF16)
    plane_copy(2).start()

    @pl.when(outer)
    def _():
        hidden_arrived(d).wait_recv()

    hidden_arrived(other_d).wait_recv()
    hidden_ref[...] = hidden_own[...]

    @pl.when(c != r)
    def _():
        first_hop().wait_send()

    for row in range(4):
        @pl.when(is_root)
        def _():
            forward(0, row, d).wait_send()

        @pl.when(is_even)
        def _():
            forward(1, row, d).wait_send()
            forward(2, row, d).wait_send()
            forward(2, row, other_d).wait_send()

    @pl.when(inner)
    def _():
        @pl.loop(0, chunks)
        def _(k):
            send_peer(k).wait_send()
            send_grads(k, half, peer, 0).wait_send()
            send_grads(k, half, pair, 1).wait_send()

            @pl.when(k < chunks - 1)
            def _():
                send_grads(k, far, pair, 2).wait_send()

        for way in range(3):
            send_hidden(way).wait_send()

    keep_tokens().wait()
    pltpu.make_async_copy(grad_gate_ref, grad_gate_ref, out_sem.at[1]).wait()
    pltpu.make_async_copy(grad_up_ref, grad_up_ref, out_sem.at[2]).wait()
    core_copy(0).wait_send()
    core_copy(1).wait_send()
    own = plane_out[0, aligned(d * rows, rows), :].astype(F32)
    for way in range(3):
        plane_copy(way).wait_recv()
        own = own + plane_in[way].astype(F32)
    grad_tokens_ref[...] = own.astype(BF16)
    for way in range(3):
        plane_copy(way).wait_send()


def exchange(tokens, gate_weight, up_weight, grad_hidden):
    rows, feats = tokens.shape
    cols = gate_weight.shape[1]
    chunks = cols // (2 * LANES)
    every = 8 * rows
    group = every // 2
    dma = pltpu.SemaphoreType.DMA
    vmem = pl.BlockSpec(memory_space=pltpu.VMEM)
    hbm = pl.BlockSpec(memory_space=pl.ANY)
    scratch = [
        pltpu.VMEM((every, feats), BF16),
        pltpu.VMEM((feats, every), BF16),
        pltpu.VMEM((chunks, feats, 2 * LANES), BF16),
        pltpu.VMEM((chunks, 2, group, 2 * LANES), BF16),
        pltpu.VMEM((chunks, 2, group, 2 * LANES), BF16),
        pltpu.VMEM((chunks, group, 2 * LANES), BF16),
        pltpu.VMEM((chunks, group, 2 * LANES), BF16),
        pltpu.VMEM((chunks, group, 2 * LANES), F32),
        pltpu.VMEM((2, group, 2 * LANES), F32),
        pltpu.VMEM((chunks, 2, group, 2 * LANES), BF16),
        pltpu.VMEM((group, cols // 2), BF16),
        pltpu.VMEM((group, cols // 2), BF16),
        pltpu.VMEM((rows, cols), BF16),
        pltpu.VMEM((every, feats), F32),
        pltpu.VMEM((every, feats), BF16),
        pltpu.VMEM((2, 2 * rows, feats), BF16),
        pltpu.VMEM((2, 2 * rows, feats), BF16),
        pltpu.VMEM((3, rows, feats), BF16),
        dma((2, chunks)),
        dma((4, 8)),
        dma((8,)),
        dma((2,)),
        dma((4,)),
        dma,
        dma,
        dma((chunks, 2)),
        dma((chunks, 2)),
        dma((chunks,)),
        dma((chunks,)),
        dma((3, chunks)),
        dma((chunks, 2)),
        dma((3,)),
        dma((2,)),
        dma((3,)),
        dma((2,)),
        dma((2,)),
        dma((3,)),
        dma((3,)),
    ]
    return pl.pallas_call(
        kernel,
        out_shape=(
            jax.ShapeDtypeStruct((rows, cols), BF16),
            jax.ShapeDtypeStruct((rows, feats), BF16),
            jax.ShapeDtypeStruct((feats, every), BF16),
            jax.ShapeDtypeStruct((every, cols // 2), BF16),
            jax.ShapeDtypeStruct((every, cols // 2), BF16),
        ),
        in_specs=[hbm, hbm, hbm, hbm],
        out_specs=(vmem, vmem, hbm, hbm, hbm),
        scratch_shapes=scratch,
        compiler_params=pltpu.CompilerParams(
            collective_id=0, has_side_effects=True, vmem_limit_bytes=60 * 2**20
        ),
        cost_estimate=pl.CostEstimate(
            flops=8 * every * feats * cols // 2, bytes_accessed=4 * feats * cols,
            transcendentals=group * cols // 2,
        ),
    )(tokens, gate_weight, up_weight, grad_hidden)


def weight_kernel(
    tokens_ref, gate_ref, up_ref, hidden_ref, grad_tokens_ref,
    hidden_out, grad_tokens_out, gate_out, up_out,
    tokens, gate, up, hidden, grad_tokens, made, sem, load_sem, grads_sem, carry_sem,
):
    width = 2 * LANES
    tiles = gate.shape[1] // width
    steps, step = made.shape[1:3]
    part = step // 2
    outs = (gate_out, up_out)
    carried = (
        (hidden_ref, hidden, hidden_out),
        (grad_tokens_ref, grad_tokens, grad_tokens_out),
    )

    def load_tokens(at):
        rows = pl.ds(at * step, step)
        return pltpu.make_async_copy(
            tokens_ref.at[rows, :], tokens.at[rows, :], load_sem.at[at]
        )

    def load_grads(which, at):
        cols = pl.ds(at * width, width)
        source, held = ((gate_ref, gate), (up_ref, up))[which]
        return pltpu.make_async_copy(
            source.at[:, cols], held.at[:, cols], grads_sem.at[which, at]
        )

    def carry(which, way):
        return pltpu.make_async_copy(
            carried[which][way], carried[which][way + 1], carry_sem.at[way, which]
        )

    def leave(at, which, piece):
        return pltpu.make_async_copy(
            made.at[which, at, pl.ds(piece * part, part), :],
            outs[which].at[pl.ds(at * step + piece * part, part), :],
            sem.at[which, at, piece],
        )

    load_tokens(0).start()
    for which in range(2):
        for tile in range(tiles):
            load_grads(which, tile).start()
    for at in range(1, steps):
        load_tokens(at).start()
    for which in range(2):
        carry(which, 0).start()
    for at in range(steps):
        load_tokens(at).wait()
        left = tokens[pl.ds(at * step, step), :]
        for which in range(2):
            if at == 0:
                for tile in range(tiles):
                    load_grads(which, tile).wait()
            made[which, at] = jnp.dot(
                left, (gate, up)[which][...], preferred_element_type=F32
            )
            for piece in range(2):
                leave(at, which, piece).start()
        if at == 0:
            for which in range(2):
                carry(which, 0).wait()
                carry(which, 1).start()
    for at in range(steps):
        for which in range(2):
            for piece in range(2):
                leave(at, which, piece).wait()
    for which in range(2):
        carry(which, 1).wait()


def weight_grads(turned_tokens, grad_gate, grad_up, hidden, grad_tokens):
    feats, every = turned_tokens.shape
    cols = grad_gate.shape[1]
    steps = 4
    shape = jax.ShapeDtypeStruct((feats, cols), F32)
    hbm = pl.BlockSpec(memory_space=pl.ANY)
    return pl.pallas_call(
        weight_kernel,
        out_shape=(
            jax.ShapeDtypeStruct(hidden.shape, hidden.dtype),
            jax.ShapeDtypeStruct(grad_tokens.shape, grad_tokens.dtype),
            shape,
            shape,
        ),
        in_specs=[hbm, hbm, hbm, hbm, hbm],
        out_specs=(hbm, hbm, hbm, hbm),
        scratch_shapes=[
            pltpu.VMEM(turned_tokens.shape, BF16),
            pltpu.VMEM(grad_gate.shape, BF16),
            pltpu.VMEM(grad_up.shape, BF16),
            pltpu.VMEM(hidden.shape, BF16),
            pltpu.VMEM(grad_tokens.shape, BF16),
            pltpu.VMEM((2, steps, feats // steps, cols), F32),
            pltpu.SemaphoreType.DMA((2, steps, 2)),
            pltpu.SemaphoreType.DMA((steps,)),
            pltpu.SemaphoreType.DMA((2, cols // (2 * LANES))),
            pltpu.SemaphoreType.DMA((2, 2)),
        ],
        compiler_params=pltpu.CompilerParams(vmem_limit_bytes=60 * 2**20),
        cost_estimate=pl.CostEstimate(
            flops=4 * every * feats * cols, bytes_accessed=8 * feats * cols, transcendentals=0
        ),
    )(turned_tokens, grad_gate, grad_up, hidden, grad_tokens)


def on_line(tokens, gate_weight, up_weight, grad_hidden):
    hidden, grad_tokens, turned_tokens, grad_gate, grad_up = exchange(
        tokens, gate_weight, up_weight, grad_hidden
    )
    return weight_grads(turned_tokens, grad_gate, grad_up, hidden, grad_tokens)


def from_root(value, axis, source):
    kept = jnp.where(lax.axis_index(axis) == source, value, 0).astype(value.dtype)
    return lax.psum(kept, axis)


def local_grads(gate_pre, up_pre, cotangent):
    sigmoid_gate = jax.nn.sigmoid(gate_pre)
    cotan_f32 = cotangent.astype(jnp.float32)
    grad_gate = (
        cotan_f32 * up_pre * sigmoid_gate * (1.0 + gate_pre * (1.0 - sigmoid_gate))
    ).astype(jnp.bfloat16)
    grad_up = (cotan_f32 * jax.nn.silu(gate_pre)).astype(jnp.bfloat16)
    return (grad_gate, grad_up)


def matmul_f32(left, right):
    return jnp.dot(left, right, preferred_element_type=jnp.float32)


def rounded_term(left, right):
    return matmul_f32(left, right).astype(jnp.bfloat16).astype(jnp.float32)


def local(tokens, gate_weight, up_weight, grad_hidden):
    hidden_cols = gate_weight.shape[1]
    row_tokens = lax.all_gather(tokens, "row", axis=0, tiled=True)
    diag_panel = from_root(row_tokens, "col", lax.axis_index("row"))
    summed = lax.psum_scatter(
        jnp.concatenate(
            [rounded_term(diag_panel, gate_weight), rounded_term(diag_panel, up_weight)], 1
        ).astype(jnp.bfloat16),
        "row",
        scatter_dimension=0,
        tiled=True,
    ).astype(jnp.float32)
    gate_sum = summed[:, :hidden_cols]
    up_sum = summed[:, hidden_cols:]
    hidden = (jax.nn.silu(gate_sum) * up_sum).astype(jnp.bfloat16)
    own_gate, own_up = local_grads(gate_sum, up_sum, grad_hidden)
    grad_gate, grad_up = (
        lax.all_gather(own_gate, "row", axis=0, tiled=True),
        lax.all_gather(own_up, "row", axis=0, tiled=True),
    )
    first_term = jnp.einsum("tf,df->td", grad_gate, gate_weight, preferred_element_type=jnp.float32)
    grad_tokens = lax.psum_scatter(
        (
            first_term
            + jnp.einsum("tf,df->td", grad_up, up_weight, preferred_element_type=jnp.float32)
        ).astype(jnp.bfloat16),
        "col",
        scatter_dimension=0,
        tiled=True,
    )
    gate_slices, up_slices = (
        lax.all_to_all(grad_gate, "depth", split_axis=1, concat_axis=0, tiled=True),
        lax.all_to_all(grad_up, "depth", split_axis=1, concat_axis=0, tiled=True),
    )
    every_tokens = lax.all_gather(diag_panel, "depth", axis=0, tiled=True)
    grad_gate_weight = jnp.einsum(
        "td,tf->df", every_tokens, gate_slices, preferred_element_type=jnp.float32
    )
    grad_up_weight = jnp.einsum(
        "td,tf->df", every_tokens, up_slices, preferred_element_type=jnp.float32
    )
    return (hidden, grad_tokens, grad_gate_weight, grad_up_weight)


def pick(mesh, tokens, gate_weight, up_weight, grad_hidden):
    sizes = dict(mesh.shape)
    fits = (
        (sizes["row"], sizes["col"], sizes["depth"]) == (4, 4, 2)
        and tokens.shape[0] % 16 == 0
        and tokens.shape[1] % 128 == 0
        and gate_weight.shape[1] % (4 * LANES) == 0
    )
    plan = on_line if fits else local
    return plan(tokens, gate_weight, up_weight, grad_hidden)


def solution(mesh):
    return jax.shard_map(
        functools.partial(pick, mesh),
        mesh=mesh,
        in_specs=(
            P(("row", "depth"), "col"),
            P("row", "col"),
            P("row", "col"),
            P(("row", "depth"), "col"),
        ),
        out_specs=(
            P(("row", "depth"), "col"),
            P(("col", "depth"), "row"),
            P("row", ("col", "depth")),
            P("row", ("col", "depth")),
        ),
        check_vma=False,
    )
```
